256 devices in a mesh: gx: 8 (over x, core), gy: 32 (over z, y).
Axes of the slice: x: 4, y: 4, z: 8, core: 2. Of those that a mesh axis runs over, the one named last changes fastest.
Arguments:
- snapshots: float32 [64, 4, 256, 4096], P(None, None, 'gx', 'gy'), may hold values from -36 to 36
- conductivity: float32 [4, 256, 4096], P(None, 'gx', 'gy'), may hold values from 0.1 to 3
- storage: float32 [4, 256, 4096], P(None, 'gx', 'gy'), may hold values from 0.5 to 2
Outputs:
- basis: float32 [64, 4, 256, 4096], P(None, None, 'gx', 'gy')
- applied: float32 [64, 4, 256, 4096], P(None, None, 'gx', 'gy')
- reduced: float32 [64, 64], replicated
The draws below stay inside these ranges and needn't reach their ends.
All inputs are finite; a program needn't handle non-finite values.
Results may differ from the reference program's by a relative error of at most 0.00025.
Values sent between devices are 32-bit elements; how exact they have to be, the bound alone decides.
A program may use at most 128 MiB of HBM per device.

```python
import math
import jax
import jax.numpy as jnp
from jax import lax

K = 64
L = 4
NX = 256
NY = 4096


def draw_snapshots(key, part):
    key = jax.random.fold_in(key, 11)
    key_rows, key_cols, key_base = jax.random.split(key, 3)
    low = math.log(0.3)
    high = math.log(3.0)
    row_scale = jnp.exp(jax.random.uniform(key_rows, (L, NX, NY), jnp.float32, low, high))
    col_scale = jnp.exp(jax.random.uniform(key_cols, (K, 1, 1, 1), jnp.float32, low, high))
    base = jax.random.truncated_normal(key_base, -4.0, 4.0, (K, L, NX, NY), jnp.float32)
    return (base * row_scale * col_scale).astype(jnp.float32)


def levels(rng, extent, cuts, smallest, top_value):
    level, own = 1.0, jax.random.fold_in(rng, 6)
    for axis_at, shards_of in cuts:
        draws = jnp.exp(jax.random.uniform(jax.random.fold_in(own, axis_at), (shards_of,), jnp.float32, smallest / len(cuts), top_value / len(cuts)))
        level = level * jnp.repeat(draws, extent[axis_at] // shards_of).reshape([-1 if axis == axis_at else 1 for axis in range(len(extent))])
    return level


def setup_inputs(seed: int = 0) -> dict:
    arg_keys = jax.random.split(jax.random.key(seed), 4)
    return {
        "snapshots": draw_snapshots(jax.random.fold_in(arg_keys[3], 71), 0),
        "conductivity": jnp.clip(jnp.exp(math.log(3.0) - 3.4011974 * jax.random.uniform(arg_keys[1], (L, NX, NY), jnp.float32) ** levels(arg_keys[1], (L, NX, NY), ((1, 8), (2, 32)), -0.2, 0.2)), 0.1, 3.0),
        "storage": jnp.clip(jnp.exp(math.log(2.0) - 1.3862944 * jax.random.uniform(arg_keys[2], (L, NX, NY), jnp.float32) ** levels(arg_keys[2], (L, NX, NY), ((1, 8), (2, 32)), -0.2, 0.2)), 0.5, 2.0),
    }


def shifted(padded, step_z, step_x, step_y):
    layer_count = padded.shape[-3] - 2
    row_count = padded.shape[-2] - 2
    column_count = padded.shape[-1] - 2
    return padded[..., 1 + step_z:1 + step_z + layer_count, 1 + step_x:1 + step_x + row_count, 1 + step_y:1 + step_y + column_count]

def apply_stencil(padded, cond_padded, storage):
    centre = shifted(padded, 0, 0, 0)
    cond_centre = shifted(cond_padded, 0, 0, 0)
    result = storage * centre
    for offset in ((1, 0, 0), (-1, 0, 0), (0, 1, 0), (0, -1, 0), (0, 0, 1), (0, 0, -1)):
        neighbour = shifted(padded, offset[0], offset[1], offset[2])
        cond_near = shifted(cond_padded, offset[0], offset[1], offset[2])
        result = result + 0.5 * (cond_centre + cond_near) * (centre - neighbour)
    return result

def reference(snapshots, conductivity, storage):
    cell_count = L * NX * NY
    flat_snap = snapshots.reshape(K, cell_count)
    gram = jnp.dot(flat_snap.astype(jnp.float32), flat_snap.T.astype(jnp.float32), precision=lax.Precision.HIGHEST, preferred_element_type=jnp.float32) / cell_count
    factor = jnp.linalg.cholesky(gram).T
    basis_flat = lax.linalg.triangular_solve(factor, flat_snap, left_side=True, lower=False, transpose_a=True)
    basis = basis_flat.reshape(snapshots.shape)
    cond_padded = jnp.pad(conductivity, 1)

    def one_column(field):
        return apply_stencil(jnp.pad(field, 1), cond_padded, storage)
    applied = lax.map(one_column, basis)
    applied_flat = applied.reshape(K, cell_count)
    reduced = jnp.dot(basis_flat.astype(jnp.float32), applied_flat.T.astype(jnp.float32), precision=lax.Precision.HIGHEST, preferred_element_type=jnp.float32) / cell_count
    return (basis, applied, reduced)
```

```python
import functools

import jax
import jax.numpy as jnp
from jax import lax
from jax.experimental import pallas as pl
from jax.experimental.pallas import tpu as pltpu
from jax.sharding import PartitionSpec as P

MESH = pl.DeviceIdType.MESH
F32 = jnp.float32
BF16 = jnp.bfloat16
K = 64
LAYERS = 4
TX = 32
TY = 128
CELLS = LAYERS * TX
XY = 16
Z = 8
COUNT = 4 * 256 * 4096


def split(value):
    high = value.astype(BF16)
    low = (value - high.astype(F32)).astype(BF16)
    return high, low


def product_nt(left, right):
    return lax.dot_general(left, right, (((1,), (1,)), ((), ())), preferred_element_type=F32)


def lanes(shape):
    return lax.broadcasted_iota(jnp.int32, shape, len(shape) - 1)


def rows(shape):
    return lax.broadcasted_iota(jnp.int32, shape, len(shape) - 2)


def folded(matrix):
    return [
        jnp.concatenate([matrix[32 * h : 32 * h + 16], matrix[32 * h + 16 : 32 * h + 32]], axis=1)
        for h in range(2)
    ]


def unfolded(halves):
    return jnp.concatenate(
        [part for h in halves for part in (h[:, :64], h[:, 64:])], axis=0
    )


class Total:
    def __init__(self, place, packed, pair, plane, column, whole, send, recv):
        self.x, self.y, self.z, self.core = place
        self.packed, self.pair, self.plane, self.column, self.whole = packed, pair, plane, column, whole
        self.send, self.recv = send, recv

    def device(self, x, y, z, core):
        return (x * 2 + core, z * 4 + y)

    def copy(self, src, dst, step, device):
        pltpu.make_async_remote_copy(
            src_ref=src,
            dst_ref=dst,
            send_sem=self.send.at[step],
            recv_sem=self.recv.at[step],
            device_id=device,
            device_id_type=MESH,
        ).start()

    def other_core(self):
        return self.device(self.x, self.y, self.z, 1 - self.core)

    def plane_peers(self):
        return [
            self.device(lax.rem(self.x + i, 4), lax.rem(self.y + j, 4), self.z, self.core)
            for i in range(4)
            for j in range(4)
            if i or j
        ]

    def column_peers(self):
        return [self.device(self.x, self.y, lax.rem(self.z + i, Z), self.core) for i in range(1, Z)]

    def start_pair(self, matrix):
        for h, half in enumerate(folded(matrix)):
            self.packed[h] = half
        self.copy(self.packed.at[1 - self.core], self.pair, 0, self.other_core())

    def start_plane(self):
        pltpu.make_async_copy(self.pair, self.pair, self.recv.at[0]).wait()
        me = self.x * 4 + self.y
        self.plane[me] = self.packed[self.core] + self.pair[...]
        for peer in self.plane_peers():
            self.copy(self.plane.at[me], self.plane.at[me], 1, peer)

    def start_column(self):
        rest = self.plane.at[pl.ds(0, XY - 1)]
        pltpu.make_async_copy(rest, rest, self.recv.at[1]).wait()
        total = self.plane[0]
        for i in range(1, XY):
            total = total + self.plane[i]
        self.column[self.z] = total
        for peer in self.column_peers():
            self.copy(self.column.at[self.z], self.column.at[self.z], 2, peer)

    def start_whole(self):
        rest = self.column.at[pl.ds(0, Z - 1)]
        pltpu.make_async_copy(rest, rest, self.recv.at[2]).wait()
        total = self.column[0]
        for i in range(1, Z):
            total = total + self.column[i]
        self.whole[self.core] = total
        self.copy(self.whole.at[self.core], self.whole.at[self.core], 3, self.other_core())

    def result(self):
        pltpu.make_async_copy(self.whole.at[0], self.whole.at[0], self.recv.at[3]).wait()
        return unfolded([self.whole[0], self.whole[1]])

    def drain(self):
        for step, ref in enumerate(
            (
                self.pair,
                self.plane.at[pl.ds(0, XY - 1)],
                self.column.at[pl.ds(0, Z - 1)],
                self.whole.at[0],
            )
        ):
            pltpu.make_async_copy(ref, ref, self.send.at[step]).wait()


def eliminated(matrix):
    eye = (rows((K, K)) == lanes((K, K))).astype(F32)
    whole = jnp.concatenate([matrix, eye], axis=1)
    blocks = [whole[8 * i : 8 * i + 8] for i in range(8)]
    sub = rows((8, 2 * K))
    for b in range(8):
        columns = [
            {i: jnp.broadcast_to(blocks[i][:, 8 * b + c : 8 * b + c + 1], (8, 2 * K)) for i in range(b, 8)}
            for c in range(8)
        ]
        for c in range(8):
            pivot = jnp.broadcast_to(columns[c][b][c : c + 1], (8, 2 * K))
            inverse = 1.0 / pivot
            pivot_row = jnp.broadcast_to(blocks[b][c : c + 1], (8, 2 * K))
            later = [jnp.broadcast_to(columns[d][b][c : c + 1], (8, 2 * K)) for d in range(c + 1, 8)]
            for i in range(b, 8):
                factor = columns[c][i] * inverse
                if i == b:
                    factor = jnp.where(sub > c, factor, 0.0)
                for at, d in enumerate(range(c + 1, 8)):
                    columns[d][i] = columns[d][i] - factor * later[at]
                blocks[i] = blocks[i] - factor * pivot_row
    whole = jnp.concatenate(blocks, axis=0)
    diagonal = rows((K, 2 * K)) == lanes((K, 2 * K))
    pivots = jnp.sum(jnp.where(diagonal, whole, 0.0), axis=1, keepdims=True)
    return whole[:, K:] * (1.0 / jnp.sqrt(pivots))


def gather_kernel(
    snap_any, cond_any, stor_any,
    snap_out, flux_out, weights_out, reduced_out,
    natural, field, cond, stor, padded, coefs, edges, flat,
    gram_acc, proj_acc,
    side_send, side_cond_send, side_cond, end_send, end_got,
    g_packed, g_pair, g_plane, g_column, g_whole,
    m_packed, m_pair, m_plane, m_column, m_whole,
    load_sem, halo_send, halo_recv, g_send, g_recv, m_send, m_recv,
):
    gx, gy = lax.axis_index("gx"), lax.axis_index("gy")
    place = (gx // 2, lax.rem(gy, 4), gy // 4, lax.rem(gx, 2))
    gram_total = Total(place, g_packed, g_pair, g_plane, g_column, g_whole, g_send, g_recv)
    proj_total = Total(place, m_packed, m_pair, m_plane, m_column, m_whole, m_send, m_recv)

    natural3 = natural.reshape(K, CELLS, TY)
    loads = []
    for l in range(LAYERS):
        part = pl.ds(l * TX, TX)
        loads.append(pltpu.make_async_copy(snap_any.at[:, part], natural3.at[:, part], load_sem.at[l]))
    loads.append(pltpu.make_async_copy(cond_any, cond, load_sem.at[LAYERS]))
    loads.append(pltpu.make_async_copy(stor_any, stor, load_sem.at[LAYERS + 1]))
    for load in loads:
        load.start()

    x_left = (lax.rem(gx + 7, 8), gy)
    x_right = (lax.rem(gx + 1, 8), gy)
    y_left = (gx, lax.rem(gy + 31, 32))
    y_right = (gx, lax.rem(gy + 1, 32))
    barrier = pltpu.get_barrier_semaphore()
    partners = [gram_total.other_core(), *gram_total.plane_peers(), *gram_total.column_peers()]
    partners += [x_left, x_right, y_left, y_right]
    for partner in partners:
        pl.semaphore_signal(barrier, inc=1, device_id=partner, device_id_type=MESH)

    gram_acc[...] = jnp.zeros_like(gram_acc)
    proj_acc[...] = jnp.zeros_like(proj_acc)
    lane = lanes((K, TY))

    for l in range(LAYERS):
        loads[l].wait()

        def four_rows(turn, carry):
            highs, lows = [], []
            for d in range(4):
                x = turn * 4 + d
                cell = l * TX + x
                value = natural[pl.ds(cell, K, stride=CELLS), :]
                field[x + 1, l] = value
                high, low = split(value)
                snap_out[cell, 0:K] = high
                snap_out[cell, K : 2 * K] = low
                turned = pltpu.roll(value, cell, 1)
                here = (lane == cell) | (lane == lax.rem(cell + TY - 1, TY))
                edges[d % 2] = jnp.where(here, turned, edges[d % 2])
                highs.append(high)
                lows.append(low)
            high = jnp.concatenate(highs, axis=1)
            low = jnp.concatenate(lows, axis=1)
            gram_acc[...] += product_nt(jnp.concatenate([high, low], axis=0), high)
            return carry

        lax.fori_loop(0, TX // 4, four_rows, 0)

    loads[LAYERS].wait()
    loads[LAYERS + 1].wait()

    even = lax.rem(lane, 2) == 0
    end_send[0, 0:K] = jnp.where(even, edges[0], edges[1])
    end_send[1, 0:K] = jnp.where(even, edges[1], edges[0])
    lane8 = lanes((8, TY))
    ends = jnp.zeros((8, TY), F32)
    for i in range(16):
        value = cond[8 * i : 8 * i + 8, :]
        ends = jnp.where(lane8 == i, pltpu.roll(value, i, 1) if i else value, ends)
        ends = jnp.where(lane8 == 16 + i, pltpu.roll(value, 17 + i, 1), ends)
    end_send[0, K : K + 8] = ends
    end_send[1, K : K + 8] = ends
    side_cond_send[...] = jnp.zeros_like(side_cond_send)
    for l in range(LAYERS):
        side_cond_send[0, l : l + 1] = cond[l * TX : l * TX + 1, :]
        side_cond_send[1, l : l + 1] = cond[l * TX + TX - 1 : l * TX + TX, :]

    cross = gram_acc[K : 2 * K]
    gram_part = gram_acc[0:K] + (cross + cross.T)

    pl.semaphore_wait(barrier, len(partners))
    gram_total.start_pair(gram_part)

    def halo(src, dst, which, device):
        copy = pltpu.make_async_remote_copy(
            src_ref=src, dst_ref=dst, send_sem=halo_send.at[which], recv_sem=halo_recv.at[which],
            device_id=device, device_id_type=MESH,
        )
        copy.start()
        return copy

    halos = [
        halo(side_cond_send.at[0], side_cond.at[1], 0, x_left),
        halo(side_cond_send.at[1], side_cond.at[0], 1, x_right),
        halo(end_send.at[0], end_got.at[1], 2, y_left),
        halo(end_send.at[1], end_got.at[0], 3, y_right),
        halo(field.at[1], field.at[TX + 1], 4, x_left),
        halo(field.at[TX], field.at[0], 5, x_right),
    ]
    gram_total.start_plane()

    for copy in halos:
        copy.wait_recv()

    first_x, last_x = gx == 0, gx == 7
    first_y, last_y = gy == 0, gy == 31
    for l in range(LAYERS):
        padded[l, 8 : 8 + TX] = cond[l * TX : l * TX + TX, :]
        padded[l, 7:8] = jnp.where(first_x, 0.0, side_cond[0, l : l + 1])
        padded[l, 8 + TX : 9 + TX] = jnp.where(last_x, 0.0, side_cond[1, l : l + 1])
    row8 = rows((8, TY))
    for l in range(LAYERS):
        for b in range(TX // 8):
            at = l * TX + 8 * b
            i = at // 8
            here = padded[l, 8 + 8 * b : 16 + 8 * b]
            x_up = 0.5 * (here + padded[l, 9 + 8 * b : 17 + 8 * b])
            x_down = 0.5 * (here + padded[l, 7 + 8 * b : 15 + 8 * b])
            l_up = 0.5 * (here + padded[l + 1, 8 + 8 * b : 16 + 8 * b]) if l + 1 < LAYERS else 0.5 * here
            l_down = 0.5 * (here + padded[l - 1, 8 + 8 * b : 16 + 8 * b]) if l else 0.5 * here
            left = jnp.where(first_y, 0.0, pltpu.roll(end_got[0, K : K + 8], TY - 16 - i, 1))
            right = jnp.where(last_y, 0.0, pltpu.roll(end_got[1, K : K + 8], TY - 1 - i, 1))
            y_down = 0.5 * (here + jnp.where(lane8 == 0, left, pltpu.roll(here, 1, 1)))
            y_up = 0.5 * (here + jnp.where(lane8 == TY - 1, right, pltpu.roll(here, TY - 1, 1)))
            centre = stor[at : at + 8, :] + x_up + x_down + l_up + l_down + y_up + y_down
            span = slice(at, at + 8)
            coefs[0, span] = centre
            coefs[1, span] = jnp.where(last_x & (row8 == 7), 0.0, x_up) if b == TX // 8 - 1 else x_up
            coefs[2, span] = jnp.where(first_x & (row8 == 0), 0.0, x_down) if b == 0 else x_down
            coefs[3, span] = l_up
            coefs[4, span] = l_down
            coefs[5, span] = jnp.where(lane8 == TY - 1, 0.0, y_up)
            coefs[6, span] = jnp.where(lane8 == 0, 0.0, y_down)
            coefs[7, span] = jnp.where(
                lane8 == 0,
                jnp.where(first_y, 0.0, y_down),
                jnp.where(lane8 == TY - 1, jnp.where(last_y, 0.0, y_up), 0.0),
            )

    from_left = pltpu.roll(end_got[0, 0:K], 1, 1)
    from_right = pltpu.roll(end_got[1, 0:K], TY - 1, 1)
    flat[0] = jnp.where(even, from_left, from_right)
    flat[1] = jnp.where(even, from_right, from_left)

    def two_rows(turn, carry):
        for d in range(2):
            x = turn * 2 + d
            for l in range(LAYERS):
                cell = l * TX + x
                coef = [coefs[i, pl.ds(cell, 1), :] for i in range(8)]
                here = field[x + 1, l]
                value = coef[0] * here
                value = value - coef[1] * field[x + 2, l]
                value = value - coef[2] * field[x, l]
                if l + 1 < LAYERS:
                    value = value - coef[3] * field[x + 1, l + 1]
                if l:
                    value = value - coef[4] * field[x + 1, l - 1]
                value = value - coef[5] * pltpu.roll(here, TY - 1, 1)
                value = value - coef[6] * pltpu.roll(here, 1, 1)
                value = value - coef[7] * pltpu.roll(flat[d], lax.rem(TY - cell, TY), 1)
                high, low = split(value)
                flux_out[cell, 0:K] = high
                flux_out[cell, K : 2 * K] = low
        cells = [l * TX + turn * 2 + d for d in range(2) for l in range(LAYERS)]
        proj_acc[...] += product_nt(
            jnp.concatenate([snap_out[cell] for cell in cells], axis=1),
            jnp.concatenate([flux_out[cell] for cell in cells], axis=1),
        )
        return carry

    lax.fori_loop(0, TX // 4, two_rows, 0)
    gram_total.start_column()
    lax.fori_loop(TX // 4, TX // 2, two_rows, 0)
    proj_part = (
        proj_acc[0:K, 0:K] + (proj_acc[K : 2 * K, 0:K] + proj_acc[0:K, K : 2 * K]) + proj_acc[K : 2 * K, K : 2 * K]
    )
    proj_total.start_pair(proj_part)
    proj_total.start_plane()
    gram_total.start_whole()
    weights = eliminated(gram_total.result() * (1.0 / COUNT))
    high, low = split(weights)
    weights_out[...] = jnp.concatenate([high, high, low, low], axis=1)
    proj_total.start_column()
    proj_total.start_whole()
    exact = dict(precision=lax.Precision.HIGHEST, preferred_element_type=F32)
    half = jnp.dot(weights, proj_total.result(), **exact)
    reduced_out[...] = lax.dot_general(half, weights, (((1,), (1,)), ((), ())), **exact) * (1.0 / COUNT)
    for copy in halos:
        copy.wait_send()
    gram_total.drain()
    proj_total.drain()


def gathered(snapshots, conductivity, storage):
    any_spec = pl.BlockSpec(memory_space=pltpu.HBM)
    vmem_spec = pl.BlockSpec(memory_space=pltpu.VMEM)
    total = [
        pltpu.VMEM((2, 16, 128), F32),
        pltpu.VMEM((16, 128), F32),
        pltpu.VMEM((XY, 16, 128), F32),
        pltpu.VMEM((Z, 16, 128), F32),
        pltpu.VMEM((2, 16, 128), F32),
    ]
    dma = pltpu.SemaphoreType.DMA
    return pl.pallas_call(
        gather_kernel,
        out_shape=(
            pltpu.VMEM((CELLS, 2 * K, TY), BF16),
            pltpu.VMEM((CELLS, 2 * K, TY), BF16),
            pltpu.VMEM((K, 4 * K), BF16),
            pltpu.VMEM((K, K), F32),
        ),
        in_specs=[any_spec] * 3,
        out_specs=(vmem_spec,) * 4,
        scratch_shapes=[
            pltpu.VMEM((K * CELLS, TY), F32),
            pltpu.VMEM((TX + 2, LAYERS, K, TY), F32),
            pltpu.VMEM((CELLS, TY), F32),
            pltpu.VMEM((CELLS, TY), F32),
            pltpu.VMEM((LAYERS, TX + 16, TY), F32),
            pltpu.VMEM((8, CELLS, TY), F32),
            pltpu.VMEM((2, K, TY), F32),
            pltpu.VMEM((2, K, TY), F32),
            pltpu.VMEM((2 * K, K), F32),
            pltpu.VMEM((2 * K, 2 * K), F32),
            pltpu.VMEM((LAYERS // 2, 8, TY), F32),
            pltpu.VMEM((2, 8, TY), F32),
            pltpu.VMEM((2, 8, TY), F32),
            pltpu.VMEM((2, K + 8, TY), F32),
            pltpu.VMEM((2, K + 8, TY), F32),
            *total,
            *total,
            dma((LAYERS + 2,)),
            dma((6,)),
            dma((6,)),
            dma((4,)),
            dma((4,)),
            dma((4,)),
            dma((4,)),
        ],
        compiler_params=pltpu.CompilerParams(
            collective_id=0, has_side_effects=True, vmem_limit_bytes=40 * 2**20
        ),
    )(
        snapshots.reshape(K, CELLS, TY),
        conductivity.reshape(CELLS, TY),
        storage.reshape(CELLS, TY),
    )


PART = 16


def expand_kernel(snap, flux, weights, reduced_in, basis, applied, reduced, basis_held, applied_held, sems):
    reduced[...] = reduced_in[...]
    copies = []
    for part in range(CELLS // PART):

        def two_cells(turn, carry):
            cell = part * PART + turn * 2
            for source, held in ((snap, basis_held), (flux, applied_held)):
                pair = jnp.concatenate([source[cell], source[cell + 1]], axis=1)
                out = jnp.dot(
                    weights[...], jnp.concatenate([pair, pair], axis=0), preferred_element_type=F32
                )
                held[pl.ds(cell, K, stride=CELLS), :] = out[:, :TY]
                held[pl.ds(cell + 1, K, stride=CELLS), :] = out[:, TY:]
            return carry

        lax.fori_loop(0, PART // 2, two_cells, 0)
        span = pl.ds(part * PART, PART)
        for which, (held, target) in enumerate(((basis_held, basis), (applied_held, applied))):
            copy = pltpu.make_async_copy(
                held.reshape(K, CELLS, TY).at[:, span], target.at[:, span], sems.at[which, part]
            )
            copy.start()
            copies.append(copy)
    for copy in copies:
        copy.wait()


def expanded(snap, flux, weights, reduced):
    vmem_spec = pl.BlockSpec(memory_space=pltpu.VMEM)
    any_spec = pl.BlockSpec(memory_space=pltpu.HBM)
    shape = jax.ShapeDtypeStruct((K, CELLS, TY), F32)
    return pl.pallas_call(
        expand_kernel,
        out_shape=(shape, shape, jax.ShapeDtypeStruct((K, K), F32)),
        in_specs=[vmem_spec] * 4,
        out_specs=(any_spec, any_spec, vmem_spec),
        scratch_shapes=[
            pltpu.VMEM((K * CELLS, TY), F32),
            pltpu.VMEM((K * CELLS, TY), F32),
            pltpu.SemaphoreType.DMA((2, CELLS // PART)),
        ],
        compiler_params=pltpu.CompilerParams(vmem_limit_bytes=40 * 2**20),
    )(snap, flux, weights, reduced)


def per_device(snapshots, conductivity, storage):
    basis, applied, reduced = expanded(*gathered(snapshots, conductivity, storage))
    return (basis.reshape(snapshots.shape), applied.reshape(snapshots.shape), reduced)


def solution(mesh):
    return jax.shard_map(
        per_device,
        mesh=mesh,
        in_specs=(P(None, None, "gx", "gy"), P(None, "gx", "gy"), P(None, "gx", "gy")),
        out_specs=(P(None, None, "gx", "gy"), P(None, None, "gx", "gy"), P()),
        check_vma=False,
    )
```

```python
import functools

import jax
import jax.numpy as jnp
from jax import lax
from jax.experimental import pallas as pl
from jax.experimental.pallas import tpu as pltpu
from jax.sharding import PartitionSpec as P

MESH = pl.DeviceIdType.MESH
F32 = jnp.float32
BF16 = jnp.bfloat16
K = 64
LAYERS = 4
TX = 32
TY = 128
CELLS = LAYERS * TX
PITCH = CELLS + 8
XY = 16
Z = 8
COUNT = 4 * 256 * 4096


def split(value):
    high = value.astype(BF16)
    low = (value - high.astype(F32)).astype(BF16)
    return high, low


def product_nt(left, right):
    return lax.dot_general(left, right, (((1,), (1,)), ((), ())), preferred_element_type=F32)


def lanes(shape):
    return lax.broadcasted_iota(jnp.int32, shape, len(shape) - 1)


def rows(shape):
    return lax.broadcasted_iota(jnp.int32, shape, len(shape) - 2)


def folded(matrix):
    return [
        jnp.concatenate([matrix[32 * h : 32 * h + 16], matrix[32 * h + 16 : 32 * h + 32]], axis=1)
        for h in range(2)
    ]


def unfolded(halves):
    return jnp.concatenate(
        [part for h in halves for part in (h[:, :64], h[:, 64:])], axis=0
    )


class Total:
    def __init__(self, place, packed, pair, plane, column, whole, send, recv):
        self.x, self.y, self.z, self.core = place
        self.packed, self.pair, self.plane, self.column, self.whole = packed, pair, plane, column, whole
        self.send, self.recv = send, recv

    def device(self, x, y, z, core):
        return (x * 2 + core, z * 4 + y)

    def copy(self, src, dst, step, device):
        pltpu.make_async_remote_copy(
            src_ref=src,
            dst_ref=dst,
            send_sem=self.send.at[step],
            recv_sem=self.recv.at[step],
            device_id=device,
            device_id_type=MESH,
        ).start()

    def other_core(self):
        return self.device(self.x, self.y, self.z, 1 - self.core)

    def plane_peers(self):
        return [
            self.device(lax.rem(self.x + i, 4), lax.rem(self.y + j, 4), self.z, self.core)
            for i in range(4)
            for j in range(4)
            if i or j
        ]

    def column_peers(self):
        return [self.device(self.x, self.y, lax.rem(self.z + i, Z), self.core) for i in range(1, Z)]

    def start_pair(self, matrix):
        for h, half in enumerate(folded(matrix)):
            self.packed[h] = half
        self.copy(self.packed.at[1 - self.core], self.pair, 0, self.other_core())

    def start_plane(self):
        pltpu.make_async_copy(self.pair, self.pair, self.recv.at[0]).wait()
        me = self.x * 4 + self.y
        self.plane[me] = self.packed[self.core] + self.pair[...]
        for peer in self.plane_peers():
            self.copy(self.plane.at[me], self.plane.at[me], 1, peer)

    def start_column(self):
        rest = self.plane.at[pl.ds(0, XY - 1)]
        pltpu.make_async_copy(rest, rest, self.recv.at[1]).wait()
        total = self.plane[0]
        for i in range(1, XY):
            total = total + self.plane[i]
        self.column[self.z] = total
        for peer in self.column_peers():
            self.copy(self.column.at[self.z], self.column.at[self.z], 2, peer)

    def start_whole(self):
        rest = self.column.at[pl.ds(0, Z - 1)]
        pltpu.make_async_copy(rest, rest, self.recv.at[2]).wait()
        total = self.column[0]
        for i in range(1, Z):
            total = total + self.column[i]
        self.whole[self.core] = total
        self.copy(self.whole.at[self.core], self.whole.at[self.core], 3, self.other_core())

    def result(self):
        pltpu.make_async_copy(self.whole.at[0], self.whole.at[0], self.recv.at[3]).wait()
        return unfolded([self.whole[0], self.whole[1]])

    def drain(self):
        for step, ref in enumerate(
            (
                self.pair,
                self.plane.at[pl.ds(0, XY - 1)],
                self.column.at[pl.ds(0, Z - 1)],
                self.whole.at[0],
            )
        ):
            pltpu.make_async_copy(ref, ref, self.send.at[step]).wait()


def eliminated(matrix):
    eye = (rows((K, K)) == lanes((K, K))).astype(F32)
    whole = jnp.concatenate([matrix, eye], axis=1)
    blocks = [whole[8 * i : 8 * i + 8] for i in range(8)]
    sub = rows((8, 2 * K))
    for b in range(8):
        columns = [
            {i: jnp.broadcast_to(blocks[i][:, 8 * b + c : 8 * b + c + 1], (8, 2 * K)) for i in range(b, 8)}
            for c in range(8)
        ]
        for c in range(8):
            pivot = jnp.broadcast_to(columns[c][b][c : c + 1], (8, 2 * K))
            inverse = 1.0 / pivot
            pivot_row = jnp.broadcast_to(blocks[b][c : c + 1], (8, 2 * K))
            later = [jnp.broadcast_to(columns[d][b][c : c + 1], (8, 2 * K)) for d in range(c + 1, 8)]
            for i in range(b, 8):
                factor = columns[c][i] * inverse
                if i == b:
                    factor = jnp.where(sub > c, factor, 0.0)
                for at, d in enumerate(range(c + 1, 8)):
                    columns[d][i] = columns[d][i] - factor * later[at]
                blocks[i] = blocks[i] - factor * pivot_row
    whole = jnp.concatenate(blocks, axis=0)
    diagonal = rows((K, 2 * K)) == lanes((K, 2 * K))
    pivots = jnp.sum(jnp.where(diagonal, whole, 0.0), axis=1, keepdims=True)
    return whole[:, K:] * (1.0 / jnp.sqrt(pivots))


UNROLL0 = 2
UNROLL1 = 4
UNROLL2 = 4
UNROLL3 = 16


def edge_pass(l, natural, field, edges):
    lane = lanes((K, TY))

    def four_rows(turn, carry):
        kept = [edges[0], edges[1]]
        for d in range(4):
            x = turn * 4 + d
            cell = l * TX + x
            value = natural[pl.ds(cell, K, stride=PITCH), :]
            field[x + 1, l] = value
            turned = pltpu.roll(value, cell, 1)
            here = (lane == cell) | (lane == lax.rem(cell + TY - 1, TY))
            kept[d % 2] = jnp.where(here, turned, kept[d % 2])
        edges[0], edges[1] = kept
        return carry

    lax.fori_loop(0, TX // 4, four_rows, 0, unroll=UNROLL0)


def gram_pass(field, snap, gram_acc):
    def one_row(x, carry):
        highs, lows = [], []
        for l in range(LAYERS):
            cell = l * TX + x
            high, low = split(field[x + 1, l])
            snap[cell, 0:K] = high
            snap[cell, K : 2 * K] = low
            highs.append(high)
            lows.append(low)
        high = jnp.concatenate(highs, axis=1)
        low = jnp.concatenate(lows, axis=1)
        gram_acc[...] += product_nt(jnp.concatenate([high, low], axis=0), high)
        return carry

    lax.fori_loop(0, TX, one_row, 0, unroll=UNROLL1)


def expand_pass(weights, source, held):
    def two_cells(turn, carry):
        cell = turn * 2
        pair = jnp.concatenate([source[cell], source[cell + 1]], axis=1)
        out = jnp.dot(weights, jnp.concatenate([pair, pair], axis=0), preferred_element_type=F32)
        held[pl.ds(cell, K, stride=PITCH), :] = out[:, :TY]
        held[pl.ds(cell + 1, K, stride=PITCH), :] = out[:, TY:]
        return carry

    lax.fori_loop(0, CELLS // 2, two_cells, 0, unroll=UNROLL3)


def second_pass(coefs, field, flat, snap, flux, proj_acc):
    def two_rows(turn, carry):
        for d in range(2):
            x = turn * 2 + d
            for l in range(LAYERS):
                cell = l * TX + x
                coef = [coefs[i, pl.ds(cell, 1), :] for i in range(8)]
                here = field[x + 1, l]
                value = coef[0] * here
                value = value - coef[1] * field[x + 2, l]
                value = value - coef[2] * field[x, l]
                if l + 1 < LAYERS:
                    value = value - coef[3] * field[x + 1, l + 1]
                if l:
                    value = value - coef[4] * field[x + 1, l - 1]
                value = value - coef[5] * pltpu.roll(here, TY - 1, 1)
                value = value - coef[6] * pltpu.roll(here, 1, 1)
                value = value - coef[7] * pltpu.roll(flat[d], lax.rem(TY - cell, TY), 1)
                high, low = split(value)
                flux[cell, 0:K] = high
                flux[cell, K : 2 * K] = low
        cells = [l * TX + turn * 2 + d for d in range(2) for l in range(LAYERS)]
        proj_acc[...] += product_nt(
            jnp.concatenate([snap[cell] for cell in cells], axis=1),
            jnp.concatenate([flux[cell] for cell in cells], axis=1),
        )
        return carry

    lax.fori_loop(0, TX // 2, two_rows, 0, unroll=UNROLL2)


def gather_kernel(
    snap_any, cond_any, stor_any,
    basis_held, applied_held, reduced_out,
    snap, flux, natural, field, cond, stor, padded, coefs, edges, flat,
    gram_acc, proj_acc,
    side_send, side_cond_send, side_cond, end_send, end_got,
    g_packed, g_pair, g_plane, g_column, g_whole,
    m_packed, m_pair, m_plane, m_column, m_whole,
    load_sem, halo_send, halo_recv, g_send, g_recv, m_send, m_recv,
):
    gx, gy = lax.axis_index("gx"), lax.axis_index("gy")
    place = (gx // 2, lax.rem(gy, 4), gy // 4, lax.rem(gx, 2))
    gram_total = Total(place, g_packed, g_pair, g_plane, g_column, g_whole, g_send, g_recv)
    proj_total = Total(place, m_packed, m_pair, m_plane, m_column, m_whole, m_send, m_recv)

    natural3 = natural.reshape(K, PITCH, TY)
    loads = []
    for l in range(LAYERS):
        part = pl.ds(l * TX, TX)
        loads.append(pltpu.make_async_copy(snap_any.at[:, part], natural3.at[:, part], load_sem.at[l]))
    loads.append(pltpu.make_async_copy(cond_any, cond, load_sem.at[LAYERS]))
    loads.append(pltpu.make_async_copy(stor_any, stor, load_sem.at[LAYERS + 1]))
    for load in loads:
        load.start()

    x_left = (lax.rem(gx + 7, 8), gy)
    x_right = (lax.rem(gx + 1, 8), gy)
    y_left = (gx, lax.rem(gy + 31, 32))
    y_right = (gx, lax.rem(gy + 1, 32))
    barrier = pltpu.get_barrier_semaphore()
    partners = [gram_total.other_core(), *gram_total.plane_peers(), *gram_total.column_peers()]
    partners += [x_left, x_right, y_left, y_right]
    for partner in partners:
        pl.semaphore_signal(barrier, inc=1, device_id=partner, device_id_type=MESH)

    gram_acc[...] = jnp.zeros_like(gram_acc)
    proj_acc[...] = jnp.zeros_like(proj_acc)
    for l in range(LAYERS):
        loads[l].wait()
        edge_pass(l, natural, field, edges)

    loads[LAYERS].wait()

    even = lax.rem(lanes((K, TY)), 2) == 0
    end_send[0, 0:K] = jnp.where(even, edges[0], edges[1])
    end_send[1, 0:K] = jnp.where(even, edges[1], edges[0])
    lane8 = lanes((8, TY))
    ends = jnp.zeros((8, TY), F32)
    for i in range(16):
        value = cond[8 * i : 8 * i + 8, :]
        ends = jnp.where(lane8 == i, pltpu.roll(value, i, 1) if i else value, ends)
        ends = jnp.where(lane8 == 16 + i, pltpu.roll(value, 17 + i, 1), ends)
    end_send[0, K : K + 8] = ends
    end_send[1, K : K + 8] = ends
    side_cond_send[...] = jnp.zeros_like(side_cond_send)
    for l in range(LAYERS):
        side_cond_send[0, l : l + 1] = cond[l * TX : l * TX + 1, :]
        side_cond_send[1, l : l + 1] = cond[l * TX + TX - 1 : l * TX + TX, :]

    def halo(src, dst, which, device):
        copy = pltpu.make_async_remote_copy(
            src_ref=src, dst_ref=dst, send_sem=halo_send.at[which], recv_sem=halo_recv.at[which],
            device_id=device, device_id_type=MESH,
        )
        copy.start()
        return copy

    pl.semaphore_wait(barrier, len(partners))
    cond_halos = [
        halo(side_cond_send.at[0], side_cond.at[1], 0, x_left),
        halo(side_cond_send.at[1], side_cond.at[0], 1, x_right),
        halo(end_send.at[0], end_got.at[1], 2, y_left),
        halo(end_send.at[1], end_got.at[0], 3, y_right),
    ]
    field_halos = [
        halo(field.at[1], field.at[TX + 1], 4, x_left),
        halo(field.at[TX], field.at[0], 5, x_right),
    ]
    halos = cond_halos + field_halos

    gram_pass(field, snap, gram_acc)
    cross = gram_acc[K : 2 * K]
    gram_total.start_pair(gram_acc[0:K] + (cross + cross.T))
    gram_total.start_plane()

    loads[LAYERS + 1].wait()
    for copy in cond_halos:
        copy.wait_recv()

    first_x, last_x = gx == 0, gx == 7
    first_y, last_y = gy == 0, gy == 31
    for l in range(LAYERS):
        padded[l, 8 : 8 + TX] = cond[l * TX : l * TX + TX, :]
        padded[l, 7:8] = jnp.where(first_x, 0.0, side_cond[0, l : l + 1])
        padded[l, 8 + TX : 9 + TX] = jnp.where(last_x, 0.0, side_cond[1, l : l + 1])
    row8 = rows((8, TY))
    for l in range(LAYERS):
        for b in range(TX // 8):
            at = l * TX + 8 * b
            i = at // 8
            here = padded[l, 8 + 8 * b : 16 + 8 * b]
            x_up = 0.5 * (here + padded[l, 9 + 8 * b : 17 + 8 * b])
            x_down = 0.5 * (here + padded[l, 7 + 8 * b : 15 + 8 * b])
            l_up = 0.5 * (here + padded[l + 1, 8 + 8 * b : 16 + 8 * b]) if l + 1 < LAYERS else 0.5 * here
            l_down = 0.5 * (here + padded[l - 1, 8 + 8 * b : 16 + 8 * b]) if l else 0.5 * here
            left = jnp.where(first_y, 0.0, pltpu.roll(end_got[0, K : K + 8], TY - 16 - i, 1))
            right = jnp.where(last_y, 0.0, pltpu.roll(end_got[1, K : K + 8], TY - 1 - i, 1))
            y_down = 0.5 * (here + jnp.where(lane8 == 0, left, pltpu.roll(here, 1, 1)))
            y_up = 0.5 * (here + jnp.where(lane8 == TY - 1, right, pltpu.roll(here, TY - 1, 1)))
            centre = stor[at : at + 8, :] + x_up + x_down + l_up + l_down + y_up + y_down
            span = slice(at, at + 8)
            coefs[0, span] = centre
            coefs[1, span] = jnp.where(last_x & (row8 == 7), 0.0, x_up) if b == TX // 8 - 1 else x_up
            coefs[2, span] = jnp.where(first_x & (row8 == 0), 0.0, x_down) if b == 0 else x_down
            coefs[3, span] = l_up
            coefs[4, span] = l_down
            coefs[5, span] = jnp.where(lane8 == TY - 1, 0.0, y_up)
            coefs[6, span] = jnp.where(lane8 == 0, 0.0, y_down)
            coefs[7, span] = jnp.where(
                lane8 == 0,
                jnp.where(first_y, 0.0, y_down),
                jnp.where(lane8 == TY - 1, jnp.where(last_y, 0.0, y_up), 0.0),
            )

    from_left = pltpu.roll(end_got[0, 0:K], 1, 1)
    from_right = pltpu.roll(end_got[1, 0:K], TY - 1, 1)
    flat[0] = jnp.where(even, from_left, from_right)
    flat[1] = jnp.where(even, from_right, from_left)

    for copy in field_halos:
        copy.wait_recv()
    second_pass(coefs, field, flat, snap, flux, proj_acc)
    gram_total.start_column()
    proj_part = (
        proj_acc[0:K, 0:K] + (proj_acc[K : 2 * K, 0:K] + proj_acc[0:K, K : 2 * K]) + proj_acc[K : 2 * K, K : 2 * K]
    )
    proj_total.start_pair(proj_part)
    proj_total.start_plane()
    gram_total.start_whole()
    proj_total.start_column()
    weights = eliminated(gram_total.result() * (1.0 / COUNT))
    high, low = split(weights)
    wide = jnp.concatenate([high, high, low, low], axis=1)
    expand_pass(wide, snap, basis_held)
    expand_pass(wide, flux, applied_held)
    proj_total.start_whole()
    exact = dict(precision=lax.Precision.HIGHEST, preferred_element_type=F32)
    half = jnp.dot(weights, proj_total.result(), **exact)
    reduced_out[...] = lax.dot_general(half, weights, (((1,), (1,)), ((), ())), **exact) * (1.0 / COUNT)
    for copy in halos:
        copy.wait_send()
    gram_total.drain()
    proj_total.drain()


def gathered(snapshots, conductivity, storage):
    any_spec = pl.BlockSpec(memory_space=pltpu.HBM)
    vmem_spec = pl.BlockSpec(memory_space=pltpu.VMEM)
    total = [
        pltpu.VMEM((2, 16, 128), F32),
        pltpu.VMEM((16, 128), F32),
        pltpu.VMEM((XY, 16, 128), F32),
        pltpu.VMEM((Z, 16, 128), F32),
        pltpu.VMEM((2, 16, 128), F32),
    ]
    dma = pltpu.SemaphoreType.DMA
    return pl.pallas_call(
        gather_kernel,
        out_shape=(
            pltpu.VMEM((K * PITCH, TY), F32),
            pltpu.VMEM((K * PITCH, TY), F32),
            pltpu.VMEM((K, K), F32),
        ),
        in_specs=[any_spec] * 3,
        out_specs=(vmem_spec,) * 3,
        scratch_shapes=[
            pltpu.VMEM((CELLS, 2 * K, TY), BF16),
            pltpu.VMEM((CELLS, 2 * K, TY), BF16),
            pltpu.VMEM((K * PITCH, TY), F32),
            pltpu.VMEM((TX + 2, LAYERS, K, TY), F32),
            pltpu.VMEM((CELLS, TY), F32),
            pltpu.VMEM((CELLS, TY), F32),
            pltpu.VMEM((LAYERS, TX + 16, TY), F32),
            pltpu.VMEM((8, CELLS, TY), F32),
            pltpu.VMEM((2, K, TY), F32),
            pltpu.VMEM((2, K, TY), F32),
            pltpu.VMEM((2 * K, K), F32),
            pltpu.VMEM((2 * K, 2 * K), F32),
            pltpu.VMEM((LAYERS // 2, 8, TY), F32),
            pltpu.VMEM((2, 8, TY), F32),
            pltpu.VMEM((2, 8, TY), F32),
            pltpu.VMEM((2, K + 8, TY), F32),
            pltpu.VMEM((2, K + 8, TY), F32),
            *total,
            *total,
            dma((LAYERS + 2,)),
            dma((6,)),
            dma((6,)),
            dma((4,)),
            dma((4,)),
            dma((4,)),
            dma((4,)),
        ],
        compiler_params=pltpu.CompilerParams(
            collective_id=0, has_side_effects=True, vmem_limit_bytes=40 * 2**20
        ),
    )(
        pltpu.with_memory_space_constraint(snapshots.reshape(K, CELLS, TY), pltpu.HBM),
        pltpu.with_memory_space_constraint(conductivity.reshape(CELLS, TY), pltpu.HBM),
        pltpu.with_memory_space_constraint(storage.reshape(CELLS, TY), pltpu.HBM),
    )


PARTS = 4


def write_kernel(basis_held, applied_held, reduced_in, basis, applied, reduced, sems):
    copies = []
    for part in range(PARTS):
        span = pl.ds(part * (K // PARTS), K // PARTS)
        for which, (held, target) in enumerate(((basis_held, basis), (applied_held, applied))):
            copy = pltpu.make_async_copy(
                held.reshape(K, PITCH, TY).at[span, 0:CELLS], target.at[span], sems.at[which, part]
            )
            copy.start()
            copies.append(copy)
    reduced[...] = reduced_in[...]
    for copy in copies:
        copy.wait()


def written(basis_held, applied_held, reduced):
    vmem_spec = pl.BlockSpec(memory_space=pltpu.VMEM)
    hbm_spec = pl.BlockSpec(memory_space=pltpu.HBM)
    shape = jax.ShapeDtypeStruct((K, CELLS, TY), F32)
    return pl.pallas_call(
        write_kernel,
        out_shape=(shape, shape, jax.ShapeDtypeStruct((K, K), F32)),
        in_specs=[vmem_spec] * 3,
        out_specs=(hbm_spec, hbm_spec, vmem_spec),
        scratch_shapes=[pltpu.SemaphoreType.DMA((2, PARTS))],
        compiler_params=pltpu.CompilerParams(vmem_limit_bytes=16 * 2**20),
    )(basis_held, applied_held, reduced)


def per_device(snapshots, conductivity, storage):
    basis, applied, reduced = written(*gathered(snapshots, conductivity, storage))
    return (basis.reshape(snapshots.shape), applied.reshape(snapshots.shape), reduced)


def solution(mesh):
    return jax.shard_map(
        per_device,
        mesh=mesh,
        in_specs=(P(None, None, "gx", "gy"), P(None, "gx", "gy"), P(None, "gx", "gy")),
        out_specs=(P(None, None, "gx", "gy"), P(None, None, "gx", "gy"), P()),
        check_vma=False,
    )
```

```python
import functools

import jax
import jax.numpy as jnp
from jax import lax
from jax.experimental import pallas as pl
from jax.experimental.pallas import tpu as pltpu
from jax.sharding import PartitionSpec as P

MESH = pl.DeviceIdType.MESH
F32 = jnp.float32
BF16 = jnp.bfloat16
K = 64
LAYERS = 4
TX = 32
TY = 128
CELLS = LAYERS * TX
PITCH = CELLS + 8
XY = 16
Z = 8
COUNT = 4 * 256 * 4096


def split(value):
    high = value.astype(BF16)
    low = (value - high.astype(F32)).astype(BF16)
    return high, low


def product_nt(left, right):
    return lax.dot_general(left, right, (((1,), (1,)), ((), ())), preferred_element_type=F32)


def lanes(shape):
    return lax.broadcasted_iota(jnp.int32, shape, len(shape) - 1)


def rows(shape):
    return lax.broadcasted_iota(jnp.int32, shape, len(shape) - 2)


def folded(matrix):
    return [
        jnp.concatenate([matrix[32 * h : 32 * h + 16], matrix[32 * h + 16 : 32 * h + 32]], axis=1)
        for h in range(2)
    ]


def unfolded(halves):
    return jnp.concatenate(
        [part for h in halves for part in (h[:, :64], h[:, 64:])], axis=0
    )


class Total:
    def __init__(self, place, packed, pair, plane, column, whole, send, recv):
        self.x, self.y, self.z, self.core = place
        self.packed, self.pair, self.plane, self.column, self.whole = packed, pair, plane, column, whole
        self.send, self.recv = send, recv

    def device(self, x, y, z, core):
        return (x * 2 + core, z * 4 + y)

    def copy(self, src, dst, step, device):
        pltpu.make_async_remote_copy(
            src_ref=src,
            dst_ref=dst,
            send_sem=self.send.at[step],
            recv_sem=self.recv.at[step],
            device_id=device,
            device_id_type=MESH,
        ).start()

    def other_core(self):
        return self.device(self.x, self.y, self.z, 1 - self.core)

    def plane_peers(self):
        return [
            self.device(lax.rem(self.x + i, 4), lax.rem(self.y + j, 4), self.z, self.core)
            for i in range(4)
            for j in range(4)
            if i or j
        ]

    def column_peers(self):
        return [self.device(self.x, self.y, lax.rem(self.z + i, Z), self.core) for i in range(1, Z)]

    def start_pair(self, matrix):
        for h, half in enumerate(folded(matrix)):
            self.packed[h] = half
        self.copy(self.packed.at[1 - self.core], self.pair, 0, self.other_core())

    def start_plane(self):
        pltpu.make_async_copy(self.pair, self.pair, self.recv.at[0]).wait()
        me = self.x * 4 + self.y
        self.plane[me] = self.packed[self.core] + self.pair[...]
        for peer in self.plane_peers():
            self.copy(self.plane.at[me], self.plane.at[me], 1, peer)

    def start_column(self):
        rest = self.plane.at[pl.ds(0, XY - 1)]
        pltpu.make_async_copy(rest, rest, self.recv.at[1]).wait()
        total = self.plane[0]
        for i in range(1, XY):
            total = total + self.plane[i]
        self.column[self.z] = total
        for peer in self.column_peers():
            self.copy(self.column.at[self.z], self.column.at[self.z], 2, peer)

    def start_whole(self):
        rest = self.column.at[pl.ds(0, Z - 1)]
        pltpu.make_async_copy(rest, rest, self.recv.at[2]).wait()
        total = self.column[0]
        for i in range(1, Z):
            total = total + self.column[i]
        self.whole[self.core] = total
        self.copy(self.whole.at[self.core], self.whole.at[self.core], 3, self.other_core())

    def result(self):
        pltpu.make_async_copy(self.whole.at[0], self.whole.at[0], self.recv.at[3]).wait()
        return unfolded([self.whole[0], self.whole[1]])

    def drain(self):
        for step, ref in enumerate(
            (
                self.pair,
                self.plane.at[pl.ds(0, XY - 1)],
                self.column.at[pl.ds(0, Z - 1)],
                self.whole.at[0],
            )
        ):
            pltpu.make_async_copy(ref, ref, self.send.at[step]).wait()


def eliminated(matrix):
    eye = (rows((K, K)) == lanes((K, K))).astype(F32)
    whole = jnp.concatenate([matrix, eye], axis=1)
    blocks = [whole[8 * i : 8 * i + 8] for i in range(8)]
    sub = rows((8, 2 * K))
    for b in range(8):
        columns = [
            {i: jnp.broadcast_to(blocks[i][:, 8 * b + c : 8 * b + c + 1], (8, 2 * K)) for i in range(b, 8)}
            for c in range(8)
        ]
        for c in range(8):
            pivot = jnp.broadcast_to(columns[c][b][c : c + 1], (8, 2 * K))
            inverse = 1.0 / pivot
            pivot_row = jnp.broadcast_to(blocks[b][c : c + 1], (8, 2 * K))
            later = [jnp.broadcast_to(columns[d][b][c : c + 1], (8, 2 * K)) for d in range(c + 1, 8)]
            for i in range(b, 8):
                factor = columns[c][i] * inverse
                if i == b:
                    factor = jnp.where(sub > c, factor, 0.0)
                for at, d in enumerate(range(c + 1, 8)):
                    columns[d][i] = columns[d][i] - factor * later[at]
                blocks[i] = blocks[i] - factor * pivot_row
    whole = jnp.concatenate(blocks, axis=0)
    diagonal = rows((K, 2 * K)) == lanes((K, 2 * K))
    pivots = jnp.sum(jnp.where(diagonal, whole, 0.0), axis=1, keepdims=True)
    return whole[:, K:] * (1.0 / jnp.sqrt(pivots))


UNROLL0 = 8
UNROLL1 = 8
UNROLL2 = 5
UNROLL3 = 32


def edge_pass(l, natural, field, edges):
    lane = lanes((K, TY))

    def four_rows(turn, carry):
        kept = [edges[0], edges[1]]
        for d in range(4):
            x = turn * 4 + d
            cell = l * TX + x
            value = natural[pl.ds(cell, K, stride=PITCH), :]
            field[x + 1, l] = value
            turned = pltpu.roll(value, cell, 1)
            here = (lane == cell) | (lane == lax.rem(cell + TY - 1, TY))
            kept[d % 2] = jnp.where(here, turned, kept[d % 2])
        edges[0], edges[1] = kept
        return carry

    lax.fori_loop(0, TX // 4, four_rows, 0, unroll=UNROLL0)


def gram_pass(field, snap, gram_acc):
    def one_row(x, carry):
        highs, lows = [], []
        for l in range(LAYERS):
            cell = l * TX + x
            high, low = split(field[x + 1, l])
            snap[cell, 0:K] = high
            snap[cell, K : 2 * K] = low
            highs.append(high)
            lows.append(low)
        high = jnp.concatenate(highs, axis=1)
        low = jnp.concatenate(lows, axis=1)
        gram_acc[...] += product_nt(jnp.concatenate([high, low], axis=0), high)
        return carry

    lax.fori_loop(0, TX, one_row, 0, unroll=UNROLL1)


def expand_pass(weights, source, held):
    def two_cells(turn, carry):
        cell = turn * 2
        pair = jnp.concatenate([source[cell], source[cell + 1]], axis=1)
        out = jnp.dot(weights, jnp.concatenate([pair, pair], axis=0), preferred_element_type=F32)
        held[pl.ds(cell, K, stride=PITCH), :] = out[:, :TY]
        held[pl.ds(cell + 1, K, stride=PITCH), :] = out[:, TY:]
        return carry

    lax.fori_loop(0, CELLS // 2, two_cells, 0, unroll=UNROLL3)


def local_coefficients(cond, stor, coefs):
    lane, row = lanes((8, TY)), rows((8, TY))
    for l in range(LAYERS):
        for b in range(TX // 8):
            at = l * TX + 8 * b
            here = cond[at : at + 8, :]

            def face(first):
                return 0.5 * (here + cond[first : first + 8, :])

            if 8 * b + 8 < TX:
                x_up = face(at + 1)
            else:
                x_up = jnp.where(row == 7, 0.0, 0.5 * (here + pltpu.roll(here, 7, 0)))
            if b:
                x_down = face(at - 1)
            else:
                x_down = jnp.where(row == 0, 0.0, 0.5 * (here + pltpu.roll(here, 1, 0)))
            l_up = face(at + TX) if l + 1 < LAYERS else 0.5 * here
            l_down = face(at - TX) if l else 0.5 * here
            y_up = jnp.where(lane == TY - 1, 0.0, 0.5 * (here + pltpu.roll(here, TY - 1, 1)))
            y_down = jnp.where(lane == 0, 0.0, 0.5 * (here + pltpu.roll(here, 1, 1)))
            centre = stor[at : at + 8, :] + x_up + x_down + l_up + l_down + y_up + y_down
            for i, value in enumerate((centre, x_up, x_down, l_up, l_down, y_up, y_down)):
                coefs[i, at : at + 8] = value


def flux_rows(xs, coefs, field, snap, flux, proj_acc, x_faces=()):
    for at, x in enumerate(xs):
        for l in range(LAYERS):
            cell = l * TX + x
            coef = [coefs[i, pl.ds(cell, 1), :] for i in range(7)]
            here = field[x + 1, l]
            value = coef[0] * here
            if not x_faces or at == 0:
                value = value - coef[1] * field[x + 2, l]
            if not x_faces or at == 1:
                value = value - coef[2] * field[x, l]
            if l + 1 < LAYERS:
                value = value - coef[3] * field[x + 1, l + 1]
            if l:
                value = value - coef[4] * field[x + 1, l - 1]
            value = value - coef[5] * pltpu.roll(here, TY - 1, 1)
            value = value - coef[6] * pltpu.roll(here, 1, 1)
            if x_faces:
                value = value + x_faces[at](l, here)
            high, low = split(value)
            flux[cell, 0:K] = high
            flux[cell, K : 2 * K] = low
    cells = [l * TX + x for x in xs for l in range(LAYERS)]
    proj_acc[...] += product_nt(
        jnp.concatenate([snap[cell] for cell in cells], axis=1),
        jnp.concatenate([flux[cell] for cell in cells], axis=1),
    )


def second_pass(coefs, field, snap, flux, proj_acc):
    def two_rows(turn, carry):
        flux_rows((1 + 2 * turn, 2 + 2 * turn), coefs, field, snap, flux, proj_acc)
        return carry

    lax.fori_loop(0, TX // 2 - 1, two_rows, 0, unroll=UNROLL2)


def gather_kernel(
    snap_any, cond_any, stor_any,
    basis_held, flux, wide_out, rim_out, weights_out, proj_out,
    snap, natural, field, cond, stor, coefs, edges,
    gram_acc, proj_acc,
    side_send, side_got, end_send, end_got,
    g_packed, g_pair, g_plane, g_column, g_whole,
    m_packed, m_pair, m_plane, m_column, m_whole,
    load_sem, halo_send, halo_recv, g_send, g_recv, m_send, m_recv,
):
    gx, gy = lax.axis_index("gx"), lax.axis_index("gy")
    place = (gx // 2, lax.rem(gy, 4), gy // 4, lax.rem(gx, 2))
    gram_total = Total(place, g_packed, g_pair, g_plane, g_column, g_whole, g_send, g_recv)
    proj_total = Total(place, m_packed, m_pair, m_plane, m_column, m_whole, m_send, m_recv)

    natural3 = natural.reshape(K, PITCH, TY)
    loads = [
        pltpu.make_async_copy(cond_any, cond, load_sem.at[LAYERS]),
        pltpu.make_async_copy(stor_any, stor, load_sem.at[LAYERS + 1]),
    ]
    for l in range(LAYERS):
        part = pl.ds(l * TX, TX)
        loads.append(pltpu.make_async_copy(snap_any.at[:, part], natural3.at[:, part], load_sem.at[l]))
    for load in loads:
        load.start()

    x_left = (lax.rem(gx + 7, 8), gy)
    x_right = (lax.rem(gx + 1, 8), gy)
    y_left = (gx, lax.rem(gy + 31, 32))
    y_right = (gx, lax.rem(gy + 1, 32))
    barrier = pltpu.get_barrier_semaphore()
    partners = [gram_total.other_core(), *gram_total.plane_peers(), *gram_total.column_peers()]
    partners += [x_left, x_right, y_left, y_right]
    for partner in partners:
        pl.semaphore_signal(barrier, inc=1, device_id=partner, device_id_type=MESH)

    gram_acc[...] = jnp.zeros_like(gram_acc)
    proj_acc[...] = jnp.zeros_like(proj_acc)
    loads[0].wait()
    loads[1].wait()
    local_coefficients(cond, stor, coefs)

    side_send[...] = jnp.zeros_like(side_send)
    for l in range(LAYERS):
        side_send[0, l : l + 1] = cond[l * TX : l * TX + 1, :]
        side_send[1, l : l + 1] = cond[l * TX + TX - 1 : l * TX + TX, :]
    turned = cond[...].T
    end_send[0, K : K + 8] = turned[0:8]
    end_send[1, K : K + 8] = turned[TY - 8 : TY]

    for l in range(LAYERS):
        loads[2 + l].wait()
        edge_pass(l, natural, field, edges)

    even = lax.rem(lanes((K, TY)), 2) == 0
    end_send[0, 0:K] = jnp.where(even, edges[0], edges[1])
    end_send[1, 0:K] = pltpu.roll(jnp.where(even, edges[1], edges[0]), 1, 1)

    def halo(src, dst, which, device):
        copy = pltpu.make_async_remote_copy(
            src_ref=src, dst_ref=dst, send_sem=halo_send.at[which], recv_sem=halo_recv.at[which],
            device_id=device, device_id_type=MESH,
        )
        copy.start()
        return copy

    pl.semaphore_wait(barrier, len(partners))
    x_halos = [
        halo(field.at[1], field.at[TX + 1], 0, x_left),
        halo(field.at[TX], field.at[0], 1, x_right),
        halo(side_send.at[0], side_got.at[1], 2, x_left),
        halo(side_send.at[1], side_got.at[0], 3, x_right),
    ]
    y_halos = [
        halo(end_send.at[0], end_got.at[1], 4, y_left),
        halo(end_send.at[1], end_got.at[0], 5, y_right),
    ]

    gram_pass(field, snap, gram_acc)
    cross = gram_acc[K : 2 * K]
    gram_total.start_pair(gram_acc[0:K] + (cross + cross.T))
    gram_total.start_plane()

    second_pass(coefs, field, snap, flux, proj_acc)

    for copy in x_halos:
        copy.wait_recv()

    def x_face(side, row, at_rim):
        inside = jnp.where(at_rim, 0.0, 1.0)

        def added(l, here):
            own = cond[l * TX + row : l * TX + row + 1, :]
            face = 0.5 * (own + inside * side_got[side, l : l + 1])
            return face * (here - inside * field[0 if side == 0 else TX + 1, l])

        return added

    flux_rows(
        (0, TX - 1), coefs, field, snap, flux, proj_acc,
        (x_face(0, 0, gx == 0), x_face(1, TX - 1, gx == 7)),
    )

    for copy in y_halos:
        copy.wait_recv()
    left_in = jnp.where(gy == 0, 0.0, 1.0)
    right_in = jnp.where(gy == 31, 0.0, 1.0)
    left_face = 0.5 * (end_send[0, K : K + 1] + left_in * end_got[0, K + 7 : K + 8])
    right_face = 0.5 * (end_send[1, K + 7 : K + 8] + right_in * end_got[1, K : K + 1])
    rim = jnp.concatenate(
        [
            left_face * (end_send[0, 0:K] - left_in * end_got[0, 0:K]),
            right_face * (end_send[1, 0:K] - right_in * end_got[1, 0:K]),
        ],
        axis=1,
    )
    exact = dict(precision=lax.Precision.HIGHEST, preferred_element_type=F32)
    ends = jnp.concatenate([end_send[0, 0:K], end_send[1, 0:K]], axis=1)
    proj_part = lax.dot_general(ends, rim, (((1,), (1,)), ((), ())), **exact) + (
        proj_acc[0:K, 0:K] + (proj_acc[K : 2 * K, 0:K] + proj_acc[0:K, K : 2 * K]) + proj_acc[K : 2 * K, K : 2 * K]
    )
    proj_total.start_pair(proj_part)
    proj_total.start_plane()
    gram_total.start_column()
    gram_total.start_whole()
    proj_total.start_column()
    weights = eliminated(gram_total.result() * (1.0 / COUNT))
    weights_out[...] = weights
    high, low = split(weights)
    wide = jnp.concatenate([high, high, low, low], axis=1)
    wide_out[...] = wide
    rim = jnp.dot(weights, rim, **exact)
    left, right = rim[:, :TY], pltpu.roll(rim[:, TY:], TY - 1, 1)
    rim_out[0] = jnp.where(even, left, right)
    rim_out[1] = jnp.where(even, right, left)
    proj_total.start_whole()
    expand_pass(wide, snap, basis_held)
    proj_out[...] = proj_total.result()
    for copy in x_halos + y_halos:
        copy.wait_send()
    gram_total.drain()
    proj_total.drain()


def gathered(snapshots, conductivity, storage):
    any_spec = pl.BlockSpec(memory_space=pltpu.HBM)
    vmem_spec = pl.BlockSpec(memory_space=pltpu.VMEM)
    total = [
        pltpu.VMEM((2, 16, 128), F32),
        pltpu.VMEM((16, 128), F32),
        pltpu.VMEM((XY, 16, 128), F32),
        pltpu.VMEM((Z, 16, 128), F32),
        pltpu.VMEM((2, 16, 128), F32),
    ]
    dma = pltpu.SemaphoreType.DMA
    return pl.pallas_call(
        gather_kernel,
        out_shape=(
            pltpu.VMEM((K * PITCH, TY), F32),
            pltpu.VMEM((CELLS, 2 * K, TY), BF16),
            pltpu.VMEM((K, 4 * K), BF16),
            pltpu.VMEM((2, K, TY), F32),
            pltpu.VMEM((K, K), F32),
            pltpu.VMEM((K, K), F32),
        ),
        in_specs=[any_spec] * 3,
        out_specs=(vmem_spec,) * 6,
        scratch_shapes=[
            pltpu.VMEM((CELLS, 2 * K, TY), BF16),
            pltpu.VMEM((K * PITCH, TY), F32),
            pltpu.VMEM((TX + 2, LAYERS, K, TY), F32),
            pltpu.VMEM((CELLS, TY), F32),
            pltpu.VMEM((CELLS, TY), F32),
            pltpu.VMEM((7, CELLS, TY), F32),
            pltpu.VMEM((2, K, TY), F32),
            pltpu.VMEM((2 * K, K), F32),
            pltpu.VMEM((2 * K, 2 * K), F32),
            pltpu.VMEM((2, 8, TY), F32),
            pltpu.VMEM((2, 8, TY), F32),
            pltpu.VMEM((2, K + 8, TY), F32),
            pltpu.VMEM((2, K + 8, TY), F32),
            *total,
            *total,
            dma((LAYERS + 2,)),
            dma((6,)),
            dma((6,)),
            dma((4,)),
            dma((4,)),
            dma((4,)),
            dma((4,)),
        ],
        compiler_params=pltpu.CompilerParams(
            collective_id=0, has_side_effects=True, vmem_limit_bytes=40 * 2**20
        ),
    )(
        pltpu.with_memory_space_constraint(snapshots.reshape(K, CELLS, TY), pltpu.HBM),
        pltpu.with_memory_space_constraint(conductivity.reshape(CELLS, TY), pltpu.HBM),
        pltpu.with_memory_space_constraint(storage.reshape(CELLS, TY), pltpu.HBM),
    )


PART = 16
BASIS_PARTS = 4


def write_kernel(
    basis_held, flux, wide, rim, weights, proj, basis, applied, reduced, applied_held, reduced_held, sems
):
    copies = []

    def out(src, dst):
        copy = pltpu.make_async_copy(src, dst, sems.at[len(copies)])
        copy.start()
        copies.append(copy)

    for part in range(BASIS_PARTS):
        span = pl.ds(part * (K // BASIS_PARTS), K // BASIS_PARTS)
        out(basis_held.reshape(K, PITCH, TY).at[span, 0:CELLS], basis.at[span])
    lane = lanes((K, TY))
    at_end = (lane == 0) | (lane == TY - 1)
    for part in range(CELLS // PART):

        def two_cells(turn, carry):
            cell = part * PART + turn * 2
            pair = jnp.concatenate([flux[cell], flux[cell + 1]], axis=1)
            both = jnp.dot(
                wide[...], jnp.concatenate([pair, pair], axis=0), preferred_element_type=F32
            )
            for d in range(2):
                ends = pltpu.roll(rim[d], lax.rem(TY - d - cell + TY, TY), 1)
                applied_held[pl.ds(cell + d, K, stride=PITCH), :] = both[
                    :, d * TY : (d + 1) * TY
                ] + jnp.where(at_end, ends, 0.0)
            return carry

        lax.fori_loop(0, PART // 2, two_cells, 0, unroll=True)
        span = pl.ds(part * PART, PART)
        out(applied_held.reshape(K, PITCH, TY).at[:, span], applied.at[:, span])
    exact = dict(precision=lax.Precision.HIGHEST, preferred_element_type=F32)
    half = jnp.dot(weights[...], proj[...], **exact)
    reduced_held[...] = lax.dot_general(half, weights[...], (((1,), (1,)), ((), ())), **exact) * (1.0 / COUNT)
    out(reduced_held, reduced)
    for copy in copies:
        copy.wait()


def written(*held):
    vmem_spec = pl.BlockSpec(memory_space=pltpu.VMEM)
    hbm_spec = pl.BlockSpec(memory_space=pltpu.HBM)
    shape = jax.ShapeDtypeStruct((K, CELLS, TY), F32)
    return pl.pallas_call(
        write_kernel,
        out_shape=(shape, shape, jax.ShapeDtypeStruct((K, K), F32)),
        in_specs=[vmem_spec] * 6,
        out_specs=(hbm_spec, hbm_spec, hbm_spec),
        scratch_shapes=[
            pltpu.VMEM((K * PITCH, TY), F32),
            pltpu.VMEM((K, K), F32),
            pltpu.SemaphoreType.DMA((BASIS_PARTS + CELLS // PART + 1,)),
        ],
        compiler_params=pltpu.CompilerParams(vmem_limit_bytes=32 * 2**20),
    )(*held)


def per_device(snapshots, conductivity, storage):
    basis, applied, reduced = written(*gathered(snapshots, conductivity, storage))
    return (basis.reshape(snapshots.shape), applied.reshape(snapshots.shape), reduced)


def solution(mesh):
    return jax.shard_map(
        per_device,
        mesh=mesh,
        in_specs=(P(None, None, "gx", "gy"), P(None, "gx", "gy"), P(None, "gx", "gy")),
        out_specs=(P(None, None, "gx", "gy"), P(None, None, "gx", "gy"), P()),
        check_vma=False,
    )
```

```python
import functools

import jax
import jax.numpy as jnp
from jax import lax
from jax.experimental import pallas as pl
from jax.experimental.pallas import tpu as pltpu
from jax.sharding import PartitionSpec as P

MESH = pl.DeviceIdType.MESH
F32 = jnp.float32
BF16 = jnp.bfloat16
K = 64
LAYERS = 4
TX = 32
TY = 128
CELLS = LAYERS * TX
PITCH = CELLS + 8
XY = 16
Z = 8
COUNT = 4 * 256 * 4096


def split(value):
    high = value.astype(BF16)
    low = (value - high.astype(F32)).astype(BF16)
    return high, low


def product_nt(left, right):
    return lax.dot_general(left, right, (((1,), (1,)), ((), ())), preferred_element_type=F32)


def lanes(shape):
    return lax.broadcasted_iota(jnp.int32, shape, len(shape) - 1)


def rows(shape):
    return lax.broadcasted_iota(jnp.int32, shape, len(shape) - 2)


SHARE = 9
HALF = K // 2


def folded(matrix):
    def laid(block, last):
        quarters = [block[8 * i : 8 * i + 8] for i in range(4)]
        return jnp.concatenate([jnp.concatenate(quarters, axis=1), last], axis=0)

    row, column = rows((HALF, HALF)), lanes((HALF, HALF))
    first, second = matrix[:HALF, :HALF], matrix[HALF:, HALF:]
    diagonal = jnp.sum(jnp.where(row == column, second, 0.0), axis=0, keepdims=True)
    none = jnp.zeros((1, 128 - HALF), F32)
    return [
        laid(matrix[:HALF, HALF:], jnp.zeros((1, 128), F32)),
        laid(jnp.where(column >= row, first, second), jnp.concatenate([diagonal, none], axis=1)),
    ]


def unfolded(shares):
    def block(share):
        return jnp.concatenate([share[0:8, HALF * i : HALF * i + HALF] for i in range(4)], axis=0)

    row, column = rows((HALF, HALF)), lanes((HALF, HALF))
    corner, both = block(shares[0]), block(shares[1])
    upper = jnp.where(column > row, both, 0.0)
    lower = jnp.where(column < row, both, 0.0)
    first = jnp.where(column >= row, both, 0.0) + upper.T
    second = lower + lower.T + jnp.where(column == row, shares[1][8:9, :HALF], 0.0)
    return jnp.concatenate(
        [jnp.concatenate([first, corner], axis=1), jnp.concatenate([corner.T, second], axis=1)], axis=0
    )


class Total:
    def __init__(self, place, packed, pair, plane, column, whole, send, recv):
        self.x, self.y, self.z, self.core = place
        self.packed, self.pair, self.plane, self.column, self.whole = packed, pair, plane, column, whole
        self.send, self.recv = send, recv

    def device(self, x, y, z, core):
        return (x * 2 + core, z * 4 + y)

    def copy(self, src, dst, step, device):
        pltpu.make_async_remote_copy(
            src_ref=src,
            dst_ref=dst,
            send_sem=self.send.at[step],
            recv_sem=self.recv.at[step],
            device_id=device,
            device_id_type=MESH,
        ).start()

    def other_core(self):
        return self.device(self.x, self.y, self.z, 1 - self.core)

    def plane_peers(self):
        return [
            self.device(lax.rem(self.x + i, 4), lax.rem(self.y + j, 4), self.z, self.core)
            for i in range(4)
            for j in range(4)
            if i or j
        ]

    def column_peers(self):
        return [self.device(self.x, self.y, lax.rem(self.z + i, Z), self.core) for i in range(1, Z)]

    def start_pair(self, matrix):
        for h, half in enumerate(folded(matrix)):
            self.packed[h] = half
        self.copy(self.packed.at[1 - self.core], self.pair, 0, self.other_core())

    def start_plane(self):
        pltpu.make_async_copy(self.pair, self.pair, self.recv.at[0]).wait()
        me = self.x * 4 + self.y
        self.plane[me] = self.packed[self.core] + self.pair[...]
        for peer in self.plane_peers():
            self.copy(self.plane.at[me], self.plane.at[me], 1, peer)

    def start_column(self):
        rest = self.plane.at[pl.ds(0, XY - 1)]
        pltpu.make_async_copy(rest, rest, self.recv.at[1]).wait()
        total = self.plane[0]
        for i in range(1, XY):
            total = total + self.plane[i]
        self.column[self.z] = total
        for peer in self.column_peers():
            self.copy(self.column.at[self.z], self.column.at[self.z], 2, peer)

    def start_whole(self):
        rest = self.column.at[pl.ds(0, Z - 1)]
        pltpu.make_async_copy(rest, rest, self.recv.at[2]).wait()
        total = self.column[0]
        for i in range(1, Z):
            total = total + self.column[i]
        self.whole[self.core] = total
        self.copy(self.whole.at[self.core], self.whole.at[self.core], 3, self.other_core())

    def result(self):
        pltpu.make_async_copy(self.whole.at[0], self.whole.at[0], self.recv.at[3]).wait()
        return unfolded([self.whole[0], self.whole[1]])

    def drain(self):
        for step, ref in enumerate(
            (
                self.pair,
                self.plane.at[pl.ds(0, XY - 1)],
                self.column.at[pl.ds(0, Z - 1)],
                self.whole.at[0],
            )
        ):
            pltpu.make_async_copy(ref, ref, self.send.at[step]).wait()


def eliminated(matrix):
    eye = (rows((K, K)) == lanes((K, K))).astype(F32)
    whole = jnp.concatenate([matrix, eye], axis=1)
    blocks = [whole[8 * i : 8 * i + 8] for i in range(8)]
    sub = rows((8, 2 * K))
    for b in range(8):
        columns = [
            {i: jnp.broadcast_to(blocks[i][:, 8 * b + c : 8 * b + c + 1], (8, 2 * K)) for i in range(b, 8)}
            for c in range(8)
        ]
        for c in range(8):
            pivot = jnp.broadcast_to(columns[c][b][c : c + 1], (8, 2 * K))
            inverse = 1.0 / pivot
            pivot_row = jnp.broadcast_to(blocks[b][c : c + 1], (8, 2 * K))
            later = [jnp.broadcast_to(columns[d][b][c : c + 1], (8, 2 * K)) for d in range(c + 1, 8)]
            for i in range(b, 8):
                factor = columns[c][i] * inverse
                if i == b:
                    factor = jnp.where(sub > c, factor, 0.0)
                for at, d in enumerate(range(c + 1, 8)):
                    columns[d][i] = columns[d][i] - factor * later[at]
                blocks[i] = blocks[i] - factor * pivot_row
    whole = jnp.concatenate(blocks, axis=0)
    diagonal = rows((K, 2 * K)) == lanes((K, 2 * K))
    pivots = jnp.sum(jnp.where(diagonal, whole, 0.0), axis=1, keepdims=True)
    return whole[:, K:] * (1.0 / jnp.sqrt(pivots))


def first_pass(first, natural, field, snap, edges, gram_acc):
    lane = lanes((K, TY))

    def two_rows(turn, carry):
        highs, lows = [], []
        for d in range(2):
            x = first + turn * 2 + d
            kept = edges[d]
            for l in range(LAYERS):
                cell = l * TX + x
                value = natural[pl.ds(cell, K, stride=PITCH), :]
                field[x + 1, l] = value
                here = (lane == cell) | (lane == lax.rem(cell + TY - 1, TY))
                kept = jnp.where(here, pltpu.roll(value, cell, 1), kept)
                high, low = split(value)
                snap[cell, 0:K] = high
                snap[cell, K : 2 * K] = low
                highs.append(high)
                lows.append(low)
            edges[d] = kept
        high = jnp.concatenate(highs, axis=1)
        low = jnp.concatenate(lows, axis=1)
        gram_acc[...] += product_nt(jnp.concatenate([high, low], axis=0), high)
        return carry

    lax.fori_loop(0, 4, two_rows, 0, unroll=True)


def expand_pass(weights, source, held):
    def two_cells(turn, carry):
        cell = turn * 2
        pair = jnp.concatenate([source[cell], source[cell + 1]], axis=1)
        out = jnp.dot(weights, jnp.concatenate([pair, pair], axis=0), preferred_element_type=F32)
        held[pl.ds(cell, K, stride=PITCH), :] = out[:, :TY]
        held[pl.ds(cell + 1, K, stride=PITCH), :] = out[:, TY:]
        return carry

    lax.fori_loop(0, CELLS // 2, two_cells, 0, unroll=True)


def local_coefficients(cond, stor, coefs):
    lane, row = lanes((8, TY)), rows((8, TY))
    for l in range(LAYERS):
        for b in range(TX // 8):
            at = l * TX + 8 * b
            here = cond[at : at + 8, :]

            def face(first):
                return 0.5 * (here + cond[first : first + 8, :])

            if 8 * b + 8 < TX:
                x_up = face(at + 1)
            else:
                x_up = jnp.where(row == 7, 0.0, 0.5 * (here + pltpu.roll(here, 7, 0)))
            if b:
                x_down = face(at - 1)
            else:
                x_down = jnp.where(row == 0, 0.0, 0.5 * (here + pltpu.roll(here, 1, 0)))
            l_up = face(at + TX) if l + 1 < LAYERS else 0.5 * here
            l_down = face(at - TX) if l else 0.5 * here
            y_up = jnp.where(lane == TY - 1, 0.0, 0.5 * (here + pltpu.roll(here, TY - 1, 1)))
            y_down = jnp.where(lane == 0, 0.0, 0.5 * (here + pltpu.roll(here, 1, 1)))
            centre = stor[at : at + 8, :] + x_up + x_down + l_up + l_down + y_up + y_down
            for i, value in enumerate((centre, x_up, x_down, l_up, l_down, y_up, y_down)):
                coefs[i, at : at + 8] = value


def flux_rows(xs, coefs, field, snap, flux, proj_acc, x_faces=()):
    for at, x in enumerate(xs):
        for l in range(LAYERS):
            cell = l * TX + x
            coef = [coefs[i, pl.ds(cell, 1), :] for i in range(7)]
            here = field[x + 1, l]
            value = coef[0] * here
            if not x_faces or at == 0:
                value = value - coef[1] * field[x + 2, l]
            if not x_faces or at == 1:
                value = value - coef[2] * field[x, l]
            if l + 1 < LAYERS:
                value = value - coef[3] * field[x + 1, l + 1]
            if l:
                value = value - coef[4] * field[x + 1, l - 1]
            value = value - coef[5] * pltpu.roll(here, TY - 1, 1)
            value = value - coef[6] * pltpu.roll(here, 1, 1)
            if x_faces:
                value = value + x_faces[at](l, here)
            high, low = split(value)
            flux[cell, 0:K] = high
            flux[cell, K : 2 * K] = low
    cells = [l * TX + x for x in xs for l in range(LAYERS)]
    proj_acc[...] += product_nt(
        jnp.concatenate([snap[cell] for cell in cells], axis=1),
        jnp.concatenate([flux[cell] for cell in cells], axis=1),
    )


def second_pass(first, last, coefs, field, snap, flux, proj_acc):
    def two_rows(turn, carry):
        flux_rows((1 + 2 * turn, 2 + 2 * turn), coefs, field, snap, flux, proj_acc)
        return carry

    lax.fori_loop(first, last, two_rows, 0, unroll=True)


def gather_kernel(
    snap_any, cond_any, stor_any,
    basis_held, flux, wide_out, rim_out, weights_out, proj_out,
    snap, natural, field, cond, stor, coefs, edges,
    gram_acc, proj_acc,
    side_send, side_got, end_send, end_got,
    g_packed, g_pair, g_plane, g_column, g_whole,
    m_packed, m_pair, m_plane, m_column, m_whole,
    load_sem, halo_send, halo_recv, g_send, g_recv, m_send, m_recv,
):
    gx, gy = lax.axis_index("gx"), lax.axis_index("gy")
    place = (gx // 2, lax.rem(gy, 4), gy // 4, lax.rem(gx, 2))
    gram_total = Total(place, g_packed, g_pair, g_plane, g_column, g_whole, g_send, g_recv)
    proj_total = Total(place, m_packed, m_pair, m_plane, m_column, m_whole, m_send, m_recv)

    natural3 = natural.reshape(K, PITCH, TY)
    loads = [
        pltpu.make_async_copy(cond_any, cond, load_sem.at[16]),
        pltpu.make_async_copy(stor_any, stor, load_sem.at[17]),
    ]
    order = (0, 3, 1, 2)
    for b in order:
        for l in range(LAYERS):
            part = pl.ds(l * TX + 8 * b, 8)
            loads.append(
                pltpu.make_async_copy(snap_any.at[:, part], natural3.at[:, part], load_sem.at[l * 4 + b])
            )
    for load in loads:
        load.start()

    x_left = (lax.rem(gx + 7, 8), gy)
    x_right = (lax.rem(gx + 1, 8), gy)
    y_left = (gx, lax.rem(gy + 31, 32))
    y_right = (gx, lax.rem(gy + 1, 32))
    barrier = pltpu.get_barrier_semaphore()
    partners = [gram_total.other_core(), *gram_total.plane_peers(), *gram_total.column_peers()]
    partners += [x_left, x_right, y_left, y_right]
    for partner in partners:
        pl.semaphore_signal(barrier, inc=1, device_id=partner, device_id_type=MESH)

    gram_acc[...] = jnp.zeros_like(gram_acc)
    proj_acc[...] = jnp.zeros_like(proj_acc)
    loads[0].wait()
    loads[1].wait()
    local_coefficients(cond, stor, coefs)

    side_send[...] = jnp.zeros_like(side_send)
    for l in range(LAYERS):
        side_send[0, l : l + 1] = cond[l * TX : l * TX + 1, :]
        side_send[1, l : l + 1] = cond[l * TX + TX - 1 : l * TX + TX, :]
    turned = cond[...].T
    end_send[0, K : K + 8] = turned[0:8]
    end_send[1, K : K + 8] = turned[TY - 8 : TY]

    def halo(src, dst, which, device):
        copy = pltpu.make_async_remote_copy(
            src_ref=src, dst_ref=dst, send_sem=halo_send.at[which], recv_sem=halo_recv.at[which],
            device_id=device, device_id_type=MESH,
        )
        copy.start()
        return copy

    for at, b in enumerate(order):
        if at == 3:
            pl.semaphore_wait(barrier, len(partners))
            x_halos = [
                halo(field.at[1], field.at[TX + 1], 0, x_left),
                halo(field.at[TX], field.at[0], 1, x_right),
                halo(side_send.at[0], side_got.at[1], 2, x_left),
                halo(side_send.at[1], side_got.at[0], 3, x_right),
            ]
        for l in range(LAYERS):
            loads[2 + at * LAYERS + l].wait()
        first_pass(8 * b, natural, field, snap, edges, gram_acc)

    cross = gram_acc[K : 2 * K]
    gram_total.start_pair(gram_acc[0:K] + (cross + cross.T))

    even = lax.rem(lanes((K, TY)), 2) == 0
    end_send[0, 0:K] = jnp.where(even, edges[0], edges[1])
    end_send[1, 0:K] = pltpu.roll(jnp.where(even, edges[1], edges[0]), 1, 1)

    y_halos = [
        halo(end_send.at[0], end_got.at[1], 4, y_left),
        halo(end_send.at[1], end_got.at[0], 5, y_right),
    ]
    second_pass(0, 5, coefs, field, snap, flux, proj_acc)
    gram_total.start_plane()
    second_pass(5, TX // 2 - 1, coefs, field, snap, flux, proj_acc)

    for copy in x_halos:
        copy.wait_recv()

    def x_face(side, row, at_rim):
        inside = jnp.where(at_rim, 0.0, 1.0)

        def added(l, here):
            own = cond[l * TX + row : l * TX + row + 1, :]
            face = 0.5 * (own + inside * side_got[side, l : l + 1])
            return face * (here - inside * field[0 if side == 0 else TX + 1, l])

        return added

    flux_rows(
        (0, TX - 1), coefs, field, snap, flux, proj_acc,
        (x_face(0, 0, gx == 0), x_face(1, TX - 1, gx == 7)),
    )

    for copy in y_halos:
        copy.wait_recv()
    left_in = jnp.where(gy == 0, 0.0, 1.0)
    right_in = jnp.where(gy == 31, 0.0, 1.0)
    left_face = 0.5 * (end_send[0, K : K + 1] + left_in * end_got[0, K + 7 : K + 8])
    right_face = 0.5 * (end_send[1, K + 7 : K + 8] + right_in * end_got[1, K : K + 1])
    rim = jnp.concatenate(
        [
            left_face * (end_send[0, 0:K] - left_in * end_got[0, 0:K]),
            right_face * (end_send[1, 0:K] - right_in * end_got[1, 0:K]),
        ],
        axis=1,
    )
    exact = dict(precision=lax.Precision.HIGHEST, preferred_element_type=F32)
    ends = jnp.concatenate([end_send[0, 0:K], end_send[1, 0:K]], axis=1)
    proj_part = lax.dot_general(ends, rim, (((1,), (1,)), ((), ())), **exact) + (
        proj_acc[0:K, 0:K] + (proj_acc[K : 2 * K, 0:K] + proj_acc[0:K, K : 2 * K]) + proj_acc[K : 2 * K, K : 2 * K]
    )
    proj_total.start_pair(proj_part)
    proj_total.start_plane()
    gram_total.start_column()
    proj_total.start_column()
    gram_total.start_whole()
    weights = eliminated(gram_total.result() * (1.0 / COUNT))
    weights_out[...] = weights
    high, low = split(weights)
    wide = jnp.concatenate([high, high, low, low], axis=1)
    wide_out[...] = wide
    rim = jnp.dot(weights, rim, **exact)
    left, right = rim[:, :TY], pltpu.roll(rim[:, TY:], TY - 1, 1)
    rim_out[0] = jnp.where(even, left, right)
    rim_out[1] = jnp.where(even, right, left)
    proj_total.start_whole()
    expand_pass(wide, snap, basis_held)
    proj_out[...] = proj_total.result()
    for copy in x_halos + y_halos:
        copy.wait_send()
    gram_total.drain()
    proj_total.drain()


def gathered(snapshots, conductivity, storage):
    any_spec = pl.BlockSpec(memory_space=pltpu.HBM)
    vmem_spec = pl.BlockSpec(memory_space=pltpu.VMEM)
    total = [
        pltpu.VMEM((2, SHARE, 128), F32),
        pltpu.VMEM((SHARE, 128), F32),
        pltpu.VMEM((XY, SHARE, 128), F32),
        pltpu.VMEM((Z, SHARE, 128), F32),
        pltpu.VMEM((2, SHARE, 128), F32),
    ]
    dma = pltpu.SemaphoreType.DMA
    return pl.pallas_call(
        gather_kernel,
        out_shape=(
            pltpu.VMEM((K * PITCH, TY), F32),
            pltpu.VMEM((CELLS, 2 * K, TY), BF16),
            pltpu.VMEM((K, 4 * K), BF16),
            pltpu.VMEM((2, K, TY), F32),
            pltpu.VMEM((K, K), F32),
            pltpu.VMEM((K, K), F32),
        ),
        in_specs=[any_spec] * 3,
        out_specs=(vmem_spec,) * 6,
        scratch_shapes=[
            pltpu.VMEM((CELLS, 2 * K, TY), BF16),
            pltpu.VMEM((K * PITCH, TY), F32),
            pltpu.VMEM((TX + 2, LAYERS, K, TY), F32),
            pltpu.VMEM((CELLS, TY), F32),
            pltpu.VMEM((CELLS, TY), F32),
            pltpu.VMEM((7, CELLS, TY), F32),
            pltpu.VMEM((2, K, TY), F32),
            pltpu.VMEM((2 * K, K), F32),
            pltpu.VMEM((2 * K, 2 * K), F32),
            pltpu.VMEM((2, 8, TY), F32),
            pltpu.VMEM((2, 8, TY), F32),
            pltpu.VMEM((2, K + 8, TY), F32),
            pltpu.VMEM((2, K + 8, TY), F32),
            *total,
            *total,
            dma((18,)),
            dma((6,)),
            dma((6,)),
            dma((4,)),
            dma((4,)),
            dma((4,)),
            dma((4,)),
        ],
        compiler_params=pltpu.CompilerParams(
            collective_id=0, has_side_effects=True, vmem_limit_bytes=40 * 2**20
        ),
    )(
        pltpu.with_memory_space_constraint(snapshots.reshape(K, CELLS, TY), pltpu.HBM),
        pltpu.with_memory_space_constraint(conductivity.reshape(CELLS, TY), pltpu.HBM),
        pltpu.with_memory_space_constraint(storage.reshape(CELLS, TY), pltpu.HBM),
    )


PART = 16
BASIS_PARTS = 4


def write_kernel(
    basis_held, flux, wide, rim, weights, proj, basis, applied, reduced, applied_held, reduced_held, sems
):
    copies = []

    def out(src, dst):
        copy = pltpu.make_async_copy(src, dst, sems.at[len(copies)])
        copy.start()
        copies.append(copy)

    for part in range(BASIS_PARTS):
        span = pl.ds(part * (K // BASIS_PARTS), K // BASIS_PARTS)
        out(basis_held.reshape(K, PITCH, TY).at[span, 0:CELLS], basis.at[span])
    lane = lanes((K, TY))
    at_end = (lane == 0) | (lane == TY - 1)
    for part in range(CELLS // PART):

        def two_cells(turn, carry):
            cell = part * PART + turn * 2
            pair = jnp.concatenate([flux[cell], flux[cell + 1]], axis=1)
            both = jnp.dot(
                wide[...], jnp.concatenate([pair, pair], axis=0), preferred_element_type=F32
            )
            for d in range(2):
                ends = pltpu.roll(rim[d], lax.rem(TY - d - cell + TY, TY), 1)
                applied_held[pl.ds(cell + d, K, stride=PITCH), :] = both[
                    :, d * TY : (d + 1) * TY
                ] + jnp.where(at_end, ends, 0.0)
            return carry

        lax.fori_loop(0, PART // 2, two_cells, 0, unroll=True)
        span = pl.ds(part * PART, PART)
        out(applied_held.reshape(K, PITCH, TY).at[:, span], applied.at[:, span])
    exact = dict(precision=lax.Precision.HIGHEST, preferred_element_type=F32)
    half = jnp.dot(weights[...], proj[...], **exact)
    reduced_held[...] = lax.dot_general(half, weights[...], (((1,), (1,)), ((), ())), **exact) * (1.0 / COUNT)
    out(reduced_held, reduced)
    for copy in copies:
        copy.wait()


def written(*held):
    vmem_spec = pl.BlockSpec(memory_space=pltpu.VMEM)
    hbm_spec = pl.BlockSpec(memory_space=pltpu.HBM)
    shape = jax.ShapeDtypeStruct((K, CELLS, TY), F32)
    return pl.pallas_call(
        write_kernel,
        out_shape=(shape, shape, jax.ShapeDtypeStruct((K, K), F32)),
        in_specs=[vmem_spec] * 6,
        out_specs=(hbm_spec, hbm_spec, hbm_spec),
        scratch_shapes=[
            pltpu.VMEM((K * PITCH, TY), F32),
            pltpu.VMEM((K, K), F32),
            pltpu.SemaphoreType.DMA((BASIS_PARTS + CELLS // PART + 1,)),
        ],
        compiler_params=pltpu.CompilerParams(vmem_limit_bytes=32 * 2**20),
    )(*held)


def per_device(snapshots, conductivity, storage):
    basis, applied, reduced = written(*gathered(snapshots, conductivity, storage))
    return (basis.reshape(snapshots.shape), applied.reshape(snapshots.shape), reduced)


def solution(mesh):
    return jax.shard_map(
        per_device,
        mesh=mesh,
        in_specs=(P(None, None, "gx", "gy"), P(None, "gx", "gy"), P(None, "gx", "gy")),
        out_specs=(P(None, None, "gx", "gy"), P(None, None, "gx", "gy"), P()),
        check_vma=False,
    )
```

```python
import functools

import jax
import jax.numpy as jnp
from jax import lax
from jax.experimental import pallas as pl
from jax.experimental.pallas import tpu as pltpu
from jax.sharding import PartitionSpec as P

MESH = pl.DeviceIdType.MESH
F32 = jnp.float32
BF16 = jnp.bfloat16
K = 64
LAYERS = 4
TX = 32
TY = 128
CELLS = LAYERS * TX
PITCH = CELLS + 8
XY = 16
Z = 8
COUNT = 4 * 256 * 4096


def split(value):
    high = value.astype(BF16)
    low = (value - high.astype(F32)).astype(BF16)
    return high, low


def product_nt(left, right):
    return lax.dot_general(left, right, (((1,), (1,)), ((), ())), preferred_element_type=F32)


def lanes(shape):
    return lax.broadcasted_iota(jnp.int32, shape, len(shape) - 1)


def rows(shape):
    return lax.broadcasted_iota(jnp.int32, shape, len(shape) - 2)


SHARE = 9
HALF = K // 2


def folded(matrix):
    def laid(block, last):
        quarters = [block[8 * i : 8 * i + 8] for i in range(4)]
        return jnp.concatenate([jnp.concatenate(quarters, axis=1), last], axis=0)

    row, column = rows((HALF, HALF)), lanes((HALF, HALF))
    first, second = matrix[:HALF, :HALF], matrix[HALF:, HALF:]
    diagonal = jnp.sum(jnp.where(row == column, second, 0.0), axis=0, keepdims=True)
    none = jnp.zeros((1, 128 - HALF), F32)
    return [
        laid(matrix[:HALF, HALF:], jnp.zeros((1, 128), F32)),
        laid(jnp.where(column >= row, first, second), jnp.concatenate([diagonal, none], axis=1)),
    ]


def unfolded(shares):
    def block(share):
        return jnp.concatenate([share[0:8, HALF * i : HALF * i + HALF] for i in range(4)], axis=0)

    row, column = rows((HALF, HALF)), lanes((HALF, HALF))
    corner, both = block(shares[0]), block(shares[1])
    upper = jnp.where(column > row, both, 0.0)
    lower = jnp.where(column < row, both, 0.0)
    first = jnp.where(column >= row, both, 0.0) + upper.T
    second = lower + lower.T + jnp.where(column == row, shares[1][8:9, :HALF], 0.0)
    return jnp.concatenate(
        [jnp.concatenate([first, corner], axis=1), jnp.concatenate([corner.T, second], axis=1)], axis=0
    )


class Total:
    def __init__(self, place, packed, plane, column, send, recv):
        self.x, self.y, self.z, self.core = place
        self.packed, self.plane, self.column = packed, plane, column
        self.send, self.recv = send, recv

    def device(self, x, y, z, core):
        return (x * 2 + core, z * 4 + y)

    def copy(self, src, dst, step, device):
        pltpu.make_async_remote_copy(
            src_ref=src,
            dst_ref=dst,
            send_sem=self.send.at[step],
            recv_sem=self.recv.at[step],
            device_id=device,
            device_id_type=MESH,
        ).start()

    def plane_peers(self):
        cores = (self.core, 1 - self.core)
        return [
            (core, self.device(lax.rem(self.x + i, 4), lax.rem(self.y + j, 4), self.z, core))
            for i in range(4)
            for j in range(4)
            for at, core in enumerate(cores)
            if i or j or at
        ]

    def column_peers(self):
        return [
            self.device(self.x, self.y, lax.rem(self.z + i, Z), core)
            for i in range(Z)
            for at, core in enumerate((self.core, 1 - self.core))
            if i or at
        ]

    def start_plane(self, matrix):
        for core, share in enumerate(folded(matrix)):
            self.packed[core] = share
        me = (self.x * 4 + self.y) * 2 + self.core
        for core, peer in self.plane_peers():
            self.copy(self.packed.at[core], self.plane.at[me], 0, peer)
        self.plane[me] = self.packed[self.core]

    def start_column(self):
        rest = self.plane.at[pl.ds(0, 2 * XY - 1)]
        pltpu.make_async_copy(rest, rest, self.recv.at[0]).wait()
        total = self.plane[0]
        for i in range(1, 2 * XY):
            total = total + self.plane[i]
        me = self.core * Z + self.z
        self.column[me] = total
        for peer in self.column_peers():
            self.copy(self.column.at[me], self.column.at[me], 1, peer)

    def result(self):
        rest = self.column.at[pl.ds(0, 2 * Z - 1)]
        pltpu.make_async_copy(rest, rest, self.recv.at[1]).wait()
        shares = []
        for core in range(2):
            total = self.column[core * Z]
            for i in range(1, Z):
                total = total + self.column[core * Z + i]
            shares.append(total)
        return unfolded(shares)

    def drain(self):
        for step, ref in enumerate((self.plane.at[pl.ds(0, 2 * XY - 1)], self.column.at[pl.ds(0, 2 * Z - 1)])):
            pltpu.make_async_copy(ref, ref, self.send.at[step]).wait()


def eliminated(matrix):
    eye = (rows((K, K)) == lanes((K, K))).astype(F32)
    whole = jnp.concatenate([matrix, eye], axis=1)
    blocks = [whole[8 * i : 8 * i + 8] for i in range(8)]
    sub = rows((8, 2 * K))
    for b in range(8):
        columns = [
            {i: jnp.broadcast_to(blocks[i][:, 8 * b + c : 8 * b + c + 1], (8, 2 * K)) for i in range(b, 8)}
            for c in range(8)
        ]
        for c in range(8):
            pivot = jnp.broadcast_to(columns[c][b][c : c + 1], (8, 2 * K))
            inverse = 1.0 / pivot
            pivot_row = jnp.broadcast_to(blocks[b][c : c + 1], (8, 2 * K))
            later = [jnp.broadcast_to(columns[d][b][c : c + 1], (8, 2 * K)) for d in range(c + 1, 8)]
            for i in range(b, 8):
                factor = columns[c][i] * inverse
                if i == b:
                    factor = jnp.where(sub > c, factor, 0.0)
                for at, d in enumerate(range(c + 1, 8)):
                    columns[d][i] = columns[d][i] - factor * later[at]
                blocks[i] = blocks[i] - factor * pivot_row
    whole = jnp.concatenate(blocks, axis=0)
    diagonal = rows((K, 2 * K)) == lanes((K, 2 * K))
    pivots = jnp.sum(jnp.where(diagonal, whole, 0.0), axis=1, keepdims=True)
    return whole[:, K:] * (1.0 / jnp.sqrt(pivots))


def first_pass(first, natural, field, snap, edges, gram_acc):
    lane = lanes((K, TY))

    def two_rows(turn, carry):
        highs, lows = [], []
        for d in range(2):
            x = first + turn * 2 + d
            kept = edges[d]
            for l in range(LAYERS):
                cell = l * TX + x
                value = natural[pl.ds(cell, K, stride=PITCH), :]
                field[x + 1, l] = value
                here = (lane == cell) | (lane == lax.rem(cell + TY - 1, TY))
                kept = jnp.where(here, pltpu.roll(value, cell, 1), kept)
                high, low = split(value)
                snap[cell, 0:K] = high
                snap[cell, K : 2 * K] = low
                highs.append(high)
                lows.append(low)
            edges[d] = kept
        high = jnp.concatenate(highs, axis=1)
        low = jnp.concatenate(lows, axis=1)
        gram_acc[...] += product_nt(jnp.concatenate([high, low], axis=0), high)
        return carry

    lax.fori_loop(0, 4, two_rows, 0, unroll=True)


def expand_pass(weights, source, held):
    def two_cells(turn, carry):
        cell = turn * 2
        pair = jnp.concatenate([source[cell], source[cell + 1]], axis=1)
        out = jnp.dot(weights, jnp.concatenate([pair, pair], axis=0), preferred_element_type=F32)
        held[pl.ds(cell, K, stride=PITCH), :] = out[:, :TY]
        held[pl.ds(cell + 1, K, stride=PITCH), :] = out[:, TY:]
        return carry

    lax.fori_loop(0, CELLS // 2, two_cells, 0, unroll=True)


def local_coefficients(cond, stor, coefs):
    lane, row = lanes((8, TY)), rows((8, TY))
    for l in range(LAYERS):
        for b in range(TX // 8):
            at = l * TX + 8 * b
            here = cond[at : at + 8, :]

            def face(first):
                return 0.5 * (here + cond[first : first + 8, :])

            if 8 * b + 8 < TX:
                x_up = face(at + 1)
            else:
                x_up = jnp.where(row == 7, 0.0, 0.5 * (here + pltpu.roll(here, 7, 0)))
            if b:
                x_down = face(at - 1)
            else:
                x_down = jnp.where(row == 0, 0.0, 0.5 * (here + pltpu.roll(here, 1, 0)))
            l_up = face(at + TX) if l + 1 < LAYERS else 0.5 * here
            l_down = face(at - TX) if l else 0.5 * here
            y_up = jnp.where(lane == TY - 1, 0.0, 0.5 * (here + pltpu.roll(here, TY - 1, 1)))
            y_down = jnp.where(lane == 0, 0.0, 0.5 * (here + pltpu.roll(here, 1, 1)))
            centre = stor[at : at + 8, :] + x_up + x_down + l_up + l_down + y_up + y_down
            for i, value in enumerate((centre, x_up, x_down, l_up, l_down, y_up, y_down)):
                coefs[i, at : at + 8] = value


def flux_rows(xs, coefs, field, snap, flux, proj_acc, x_faces=()):
    for at, x in enumerate(xs):
        for l in range(LAYERS):
            cell = l * TX + x
            coef = [coefs[i, pl.ds(cell, 1), :] for i in range(7)]
            here = field[x + 1, l]
            value = coef[0] * here
            if not x_faces or at == 0:
                value = value - coef[1] * field[x + 2, l]
            if not x_faces or at == 1:
                value = value - coef[2] * field[x, l]
            if l + 1 < LAYERS:
                value = value - coef[3] * field[x + 1, l + 1]
            if l:
                value = value - coef[4] * field[x + 1, l - 1]
            value = value - coef[5] * pltpu.roll(here, TY - 1, 1)
            value = value - coef[6] * pltpu.roll(here, 1, 1)
            if x_faces:
                value = value + x_faces[at](l, here)
            high, low = split(value)
            flux[cell, 0:K] = high
            flux[cell, K : 2 * K] = low
    cells = [l * TX + x for x in xs for l in range(LAYERS)]
    proj_acc[...] += product_nt(
        jnp.concatenate([snap[cell] for cell in cells], axis=1),
        jnp.concatenate([flux[cell] for cell in cells], axis=1),
    )


def second_pass(first, last, coefs, field, snap, flux, proj_acc):
    def two_rows(turn, carry):
        flux_rows((1 + 2 * turn, 2 + 2 * turn), coefs, field, snap, flux, proj_acc)
        return carry

    lax.fori_loop(first, last, two_rows, 0, unroll=True)


def gather_kernel(
    snap_any, cond_any, stor_any,
    basis_held, flux, wide_out, rim_out, weights_out, proj_out,
    snap, natural, field, cond, stor, coefs, edges,
    gram_acc, proj_acc,
    side_send, side_got, end_send, end_got,
    g_packed, g_plane, g_column,
    m_packed, m_plane, m_column,
    load_sem, halo_send, halo_recv, g_send, g_recv, m_send, m_recv,
):
    gx, gy = lax.axis_index("gx"), lax.axis_index("gy")
    place = (gx // 2, lax.rem(gy, 4), gy // 4, lax.rem(gx, 2))
    gram_total = Total(place, g_packed, g_plane, g_column, g_send, g_recv)
    proj_total = Total(place, m_packed, m_plane, m_column, m_send, m_recv)

    natural3 = natural.reshape(K, PITCH, TY)
    loads = [
        pltpu.make_async_copy(cond_any, cond, load_sem.at[16]),
        pltpu.make_async_copy(stor_any, stor, load_sem.at[17]),
    ]
    order = (0, 3, 1, 2)
    for b in order:
        for l in range(LAYERS):
            part = pl.ds(l * TX + 8 * b, 8)
            loads.append(
                pltpu.make_async_copy(snap_any.at[:, part], natural3.at[:, part], load_sem.at[l * 4 + b])
            )
    for load in loads:
        load.start()

    x_left = (lax.rem(gx + 7, 8), gy)
    x_right = (lax.rem(gx + 1, 8), gy)
    y_left = (gx, lax.rem(gy + 31, 32))
    y_right = (gx, lax.rem(gy + 1, 32))
    barrier = pltpu.get_barrier_semaphore()
    partners = [peer for _, peer in gram_total.plane_peers()] + gram_total.column_peers()
    partners += [x_left, x_right, y_left, y_right]
    for partner in partners:
        pl.semaphore_signal(barrier, inc=1, device_id=partner, device_id_type=MESH)

    gram_acc[...] = jnp.zeros_like(gram_acc)
    proj_acc[...] = jnp.zeros_like(proj_acc)
    loads[0].wait()
    loads[1].wait()
    local_coefficients(cond, stor, coefs)

    side_send[...] = jnp.zeros_like(side_send)
    for l in range(LAYERS):
        side_send[0, l : l + 1] = cond[l * TX : l * TX + 1, :]
        side_send[1, l : l + 1] = cond[l * TX + TX - 1 : l * TX + TX, :]
    turned = cond[...].T
    end_send[0, K : K + 8] = turned[0:8]
    end_send[1, K : K + 8] = turned[TY - 8 : TY]

    def halo(src, dst, which, device):
        copy = pltpu.make_async_remote_copy(
            src_ref=src, dst_ref=dst, send_sem=halo_send.at[which], recv_sem=halo_recv.at[which],
            device_id=device, device_id_type=MESH,
        )
        copy.start()
        return copy

    for at, b in enumerate(order):
        if at == 3:
            pl.semaphore_wait(barrier, len(partners))
            x_halos = [
                halo(field.at[1], field.at[TX + 1], 0, x_left),
                halo(field.at[TX], field.at[0], 1, x_right),
                halo(side_send.at[0], side_got.at[1], 2, x_left),
                halo(side_send.at[1], side_got.at[0], 3, x_right),
            ]
        for l in range(LAYERS):
            loads[2 + at * LAYERS + l].wait()
        first_pass(8 * b, natural, field, snap, edges, gram_acc)

    cross = gram_acc[K : 2 * K]
    gram_total.start_plane(gram_acc[0:K] + (cross + cross.T))

    even = lax.rem(lanes((K, TY)), 2) == 0
    end_send[0, 0:K] = jnp.where(even, edges[0], edges[1])
    end_send[1, 0:K] = pltpu.roll(jnp.where(even, edges[1], edges[0]), 1, 1)

    y_halos = [
        halo(end_send.at[0], end_got.at[1], 4, y_left),
        halo(end_send.at[1], end_got.at[0], 5, y_right),
    ]
    second_pass(0, TX // 2 - 1, coefs, field, snap, flux, proj_acc)

    for copy in x_halos:
        copy.wait_recv()

    def x_face(side, row, at_rim):
        inside = jnp.where(at_rim, 0.0, 1.0)

        def added(l, here):
            own = cond[l * TX + row : l * TX + row + 1, :]
            face = 0.5 * (own + inside * side_got[side, l : l + 1])
            return face * (here - inside * field[0 if side == 0 else TX + 1, l])

        return added

    flux_rows(
        (0, TX - 1), coefs, field, snap, flux, proj_acc,
        (x_face(0, 0, gx == 0), x_face(1, TX - 1, gx == 7)),
    )

    for copy in y_halos:
        copy.wait_recv()
    left_in = jnp.where(gy == 0, 0.0, 1.0)
    right_in = jnp.where(gy == 31, 0.0, 1.0)
    left_face = 0.5 * (end_send[0, K : K + 1] + left_in * end_got[0, K + 7 : K + 8])
    right_face = 0.5 * (end_send[1, K + 7 : K + 8] + right_in * end_got[1, K : K + 1])
    rim = jnp.concatenate(
        [
            left_face * (end_send[0, 0:K] - left_in * end_got[0, 0:K]),
            right_face * (end_send[1, 0:K] - right_in * end_got[1, 0:K]),
        ],
        axis=1,
    )
    exact = dict(precision=lax.Precision.HIGHEST, preferred_element_type=F32)
    ends = jnp.concatenate([end_send[0, 0:K], end_send[1, 0:K]], axis=1)
    proj_part = lax.dot_general(ends, rim, (((1,), (1,)), ((), ())), **exact) + (
        proj_acc[0:K, 0:K] + (proj_acc[K : 2 * K, 0:K] + proj_acc[0:K, K : 2 * K]) + proj_acc[K : 2 * K, K : 2 * K]
    )
    proj_total.start_plane(proj_part)
    gram_total.start_column()
    proj_total.start_column()
    weights = eliminated(gram_total.result() * (1.0 / COUNT))
    weights_out[...] = weights
    high, low = split(weights)
    wide = jnp.concatenate([high, high, low, low], axis=1)
    wide_out[...] = wide
    rim = jnp.dot(weights, rim, **exact)
    left, right = rim[:, :TY], pltpu.roll(rim[:, TY:], TY - 1, 1)
    rim_out[0] = jnp.where(even, left, right)
    rim_out[1] = jnp.where(even, right, left)
    expand_pass(wide, snap, basis_held)
    proj_out[...] = proj_total.result()
    for copy in x_halos + y_halos:
        copy.wait_send()
    gram_total.drain()
    proj_total.drain()


def gathered(snapshots, conductivity, storage):
    any_spec = pl.BlockSpec(memory_space=pltpu.HBM)
    vmem_spec = pl.BlockSpec(memory_space=pltpu.VMEM)
    total = [
        pltpu.VMEM((2, SHARE, 128), F32),
        pltpu.VMEM((2 * XY, SHARE, 128), F32),
        pltpu.VMEM((2 * Z, SHARE, 128), F32),
    ]
    dma = pltpu.SemaphoreType.DMA
    return pl.pallas_call(
        gather_kernel,
        out_shape=(
            pltpu.VMEM((K * PITCH, TY), F32),
            pltpu.VMEM((CELLS, 2 * K, TY), BF16),
            pltpu.VMEM((K, 4 * K), BF16),
            pltpu.VMEM((2, K, TY), F32),
            pltpu.VMEM((K, K), F32),
            pltpu.VMEM((K, K), F32),
        ),
        in_specs=[any_spec] * 3,
        out_specs=(vmem_spec,) * 6,
        scratch_shapes=[
            pltpu.VMEM((CELLS, 2 * K, TY), BF16),
            pltpu.VMEM((K * PITCH, TY), F32),
            pltpu.VMEM((TX + 2, LAYERS, K, TY), F32),
            pltpu.VMEM((CELLS, TY), F32),
            pltpu.VMEM((CELLS, TY), F32),
            pltpu.VMEM((7, CELLS, TY), F32),
            pltpu.VMEM((2, K, TY), F32),
            pltpu.VMEM((2 * K, K), F32),
            pltpu.VMEM((2 * K, 2 * K), F32),
            pltpu.VMEM((2, 8, TY), F32),
            pltpu.VMEM((2, 8, TY), F32),
            pltpu.VMEM((2, K + 8, TY), F32),
            pltpu.VMEM((2, K + 8, TY), F32),
            *total,
            *total,
            dma((18,)),
            dma((6,)),
            dma((6,)),
            dma((2,)),
            dma((2,)),
            dma((2,)),
            dma((2,)),
        ],
        compiler_params=pltpu.CompilerParams(
            collective_id=0, has_side_effects=True, vmem_limit_bytes=40 * 2**20
        ),
    )(
        pltpu.with_memory_space_constraint(snapshots.reshape(K, CELLS, TY), pltpu.HBM),
        pltpu.with_memory_space_constraint(conductivity.reshape(CELLS, TY), pltpu.HBM),
        pltpu.with_memory_space_constraint(storage.reshape(CELLS, TY), pltpu.HBM),
    )


PART = 16
BASIS_PARTS = 4


def write_kernel(
    basis_held, flux, wide, rim, weights, proj, basis, applied, reduced, applied_held, reduced_held, sems
):
    copies = []

    def out(src, dst):
        copy = pltpu.make_async_copy(src, dst, sems.at[len(copies)])
        copy.start()
        copies.append(copy)

    for part in range(BASIS_PARTS):
        span = pl.ds(part * (K // BASIS_PARTS), K // BASIS_PARTS)
        out(basis_held.reshape(K, PITCH, TY).at[span, 0:CELLS], basis.at[span])
    lane = lanes((K, TY))
    at_end = (lane == 0) | (lane == TY - 1)
    for part in range(CELLS // PART):

        def two_cells(turn, carry):
            cell = part * PART + turn * 2
            pair = jnp.concatenate([flux[cell], flux[cell + 1]], axis=1)
            both = jnp.dot(
                wide[...], jnp.concatenate([pair, pair], axis=0), preferred_element_type=F32
            )
            for d in range(2):
                ends = pltpu.roll(rim[d], lax.rem(TY - d - cell + TY, TY), 1)
                applied_held[pl.ds(cell + d, K, stride=PITCH), :] = both[
                    :, d * TY : (d + 1) * TY
                ] + jnp.where(at_end, ends, 0.0)
            return carry

        lax.fori_loop(0, PART // 2, two_cells, 0, unroll=True)
        span = pl.ds(part * PART, PART)
        out(applied_held.reshape(K, PITCH, TY).at[:, span], applied.at[:, span])
    exact = dict(precision=lax.Precision.HIGHEST, preferred_element_type=F32)
    half = jnp.dot(weights[...], proj[...], **exact)
    reduced_held[...] = lax.dot_general(half, weights[...], (((1,), (1,)), ((), ())), **exact) * (1.0 / COUNT)
    out(reduced_held, reduced)
    for copy in copies:
        copy.wait()


def written(*held):
    vmem_spec = pl.BlockSpec(memory_space=pltpu.VMEM)
    hbm_spec = pl.BlockSpec(memory_space=pltpu.HBM)
    shape = jax.ShapeDtypeStruct((K, CELLS, TY), F32)
    return pl.pallas_call(
        write_kernel,
        out_shape=(shape, shape, jax.ShapeDtypeStruct((K, K), F32)),
        in_specs=[vmem_spec] * 6,
        out_specs=(hbm_spec, hbm_spec, hbm_spec),
        scratch_shapes=[
            pltpu.VMEM((K * PITCH, TY), F32),
            pltpu.VMEM((K, K), F32),
            pltpu.SemaphoreType.DMA((BASIS_PARTS + CELLS // PART + 1,)),
        ],
        compiler_params=pltpu.CompilerParams(vmem_limit_bytes=32 * 2**20),
    )(*held)


def per_device(snapshots, conductivity, storage):
    basis, applied, reduced = written(*gathered(snapshots, conductivity, storage))
    return (basis.reshape(snapshots.shape), applied.reshape(snapshots.shape), reduced)


def solution(mesh):
    return jax.shard_map(
        per_device,
        mesh=mesh,
        in_specs=(P(None, None, "gx", "gy"), P(None, "gx", "gy"), P(None, "gx", "gy")),
        out_specs=(P(None, None, "gx", "gy"), P(None, None, "gx", "gy"), P()),
        check_vma=False,
    )
```
